256 devices in a mesh: frame: 4 (over x), cuts: 64 (over y, z, core).
Axes of the slice: x: 4, y: 4, z: 8, core: 2. Of those that a mesh axis runs over, the one named last changes fastest.
Arguments:
- measured: float32 [64, 64, 20, 8, 512], P('frame', 'cuts'), may hold values from -6 to 6
- coil_maps: float32 [64, 20, 8, 512], P('cuts'), may hold values from -2 to 2
- sampling: int32 [64, 256], P('frame'), may hold values from 0 to 1, as said below
Outputs:
- image: float32 [64, 64, 8, 512], P('frame', 'cuts')
The draws below stay inside these ranges and needn't reach their ends.
Inputs may be any that keep to these rules, and one draw needn't show every extreme that they name: `sampling`: each frame samples between 32 and 64 of the 256 lines, always the 16 central ones; some frame samples exactly 64.
All inputs are finite; a program needn't handle non-finite values.
Results may differ from the reference program's by a relative error of at most 0.0003.
Values sent between devices are 32-bit elements; how exact they have to be, the bound alone decides.
No kernel may reach another device: no remote copies, remote signals or barrier semaphores. Data moves between devices by JAX's collectives and lax.ppermute only.
A program may use at most 128 MiB of HBM per device.

```python
import math
import jax
import jax.numpy as jnp
from jax import lax

NY = 256
COILS = 20
FRAMES = 64
XW = 8
ITERS = 2
MOST = 64
CENTER = 16
SLICES = 64


def draw_coil_maps(key, part):
    key = jax.random.fold_in(key, 11)
    key_size, key_phase = jax.random.split(key)
    depth = jnp.arange(SLICES, dtype=jnp.float32) / max(SLICES - 1, 1)
    shape = (SLICES, COILS, XW, NY)
    levels = 0.5 * jnp.power(3.2, depth)
    magnitude = jax.random.uniform(key_size, shape, jnp.float32, 0.5, 1.5)
    phases = jax.random.uniform(key_phase, shape, jnp.float32, -math.pi, math.pi)
    amplitude = levels[:, None, None, None] * magnitude / math.sqrt(COILS)
    return jnp.concatenate([amplitude * jnp.cos(phases), amplitude * jnp.sin(phases)], -1)


def draw_sampling(key, part):
    key = jax.random.fold_in(key, 23)
    key_count, key_pick, key_score = jax.random.split(key, 3)
    line_counts = jax.random.randint(key_count, (FRAMES,), MOST // 2, MOST + 1)
    fullest = jax.random.randint(key_pick, (), 0, FRAMES)
    line_counts = jnp.where(jnp.arange(FRAMES) == fullest, MOST, line_counts)
    position = jnp.arange(NY, dtype=jnp.int32)
    distance = jnp.abs(position - NY // 2)
    first_central = NY // 2 - CENTER // 2
    central = (position >= first_central) & (position < first_central + CENTER)
    random_draw = jax.random.randint(key_score, (FRAMES, NY), 0, 4096)
    scores = random_draw * (NY - distance)[None, :] * NY + position[None, :]
    scores = jnp.where(central[None, :], (1 << 30) + position[None, :], scores)
    ordering = jnp.argsort(-scores, axis=1)
    ranking = jnp.argsort(ordering, axis=1)
    return (ranking < line_counts[:, None]).astype(jnp.int32)


def steps_of(own_key, dims, pieces, low, largest):
    gain, own = 1.0, jax.random.fold_in(own_key, 6)
    for dim, parts in pieces:
        heights = jnp.exp(jax.random.uniform(jax.random.fold_in(own, dim), (parts,), jnp.float32, low / len(pieces), largest / len(pieces)))
        gain = gain * jnp.repeat(heights, dims[dim] // parts).reshape([-1 if axis == dim else 1 for axis in range(len(dims))])
    return gain


def normal_values(key, extent, width, reach, shards=(), kind=jnp.bfloat16):
    factor_of = steps_of(key, extent, shards, -0.22, 0.18) if shards else 1.0
    drawn = jax.random.normal(key, extent, jnp.float32) * width * factor_of
    return jnp.minimum(jnp.maximum(drawn, -reach), reach).astype(kind)


def setup_inputs(seed: int = 0) -> dict:
    arg_keys = jax.random.split(jax.random.key(seed), 4)
    return {
        "measured": normal_values(arg_keys[0], (FRAMES, SLICES, COILS, XW, 2 * NY), 1.0, 6.0, ((0, 4), (1, 64)), jnp.float32),
        "coil_maps": draw_coil_maps(jax.random.fold_in(arg_keys[3], 71), 0),
        "sampling": draw_sampling(jax.random.fold_in(arg_keys[3], 71), 0),
    }


TAU = 0.25
SIGMA = 0.25
LAM_TIME = 0.2
LAM_SPACE = 0.1
EPSILON = 1e-06

def complexed(field):
    return lax.complex(field[..., :NY], field[..., NY:])

def realed(field):
    return jnp.concatenate([jnp.real(field), jnp.imag(field)], -1)

def squared(field):
    return jnp.real(field) * jnp.real(field) + jnp.imag(field) * jnp.imag(field)

def forward_diff(field, axis_number):
    upper = lax.slice_in_dim(field, 1, field.shape[axis_number], axis=axis_number)
    zero_rim = jnp.zeros_like(lax.slice_in_dim(field, 0, 1, axis=axis_number))
    return jnp.concatenate([upper, zero_rim], axis_number) - field

def backward_diff(field, axis_number):
    lower = lax.slice_in_dim(field, 0, field.shape[axis_number] - 1, axis=axis_number)
    zero_rim = jnp.zeros_like(lax.slice_in_dim(field, 0, 1, axis=axis_number))
    return jnp.concatenate([zero_rim, lower], axis_number) - field

def reference(measured, coil_maps, sampling):
    complex_maps = complexed(coil_maps)
    frame_weight = sampling.astype(jnp.float32)

    def adjoint_frame(operands):
        frame_data, weight_row = operands
        coil_images = jnp.fft.ifft(complexed(frame_data) * weight_row, axis=-1, norm='ortho')
        return realed(lax.optimization_barrier(jnp.sum(jnp.conj(complex_maps) * coil_images, axis=1)))

    def data_frame(operands):
        frame_dual, frame_data, weight_row, frame_image = operands
        kspace = jnp.fft.fft(complex_maps * complexed(frame_image)[:, None], axis=-1, norm='ortho') * weight_row
        doubled = jnp.concatenate([weight_row, weight_row])
        updated = (frame_dual + SIGMA * (realed(kspace) - frame_data * doubled)) / (1.0 + SIGMA)
        coil_images = jnp.fft.ifft(complexed(updated) * weight_row, axis=-1, norm='ortho')
        return (updated, realed(lax.optimization_barrier(jnp.sum(jnp.conj(complex_maps) * coil_images, axis=1))))
    initial = lax.map(adjoint_frame, (measured, frame_weight))
    energy = jnp.sum(initial * initial)
    rms_level = jnp.sqrt(energy / (FRAMES * SLICES * XW * NY) + EPSILON)
    limit_time = LAM_TIME * rms_level
    limit_space = LAM_SPACE * rms_level
    image = initial
    image_bar = initial
    data_dual = jnp.zeros_like(measured)
    time_dual = jnp.zeros_like(complexed(initial))
    space_dual = [jnp.zeros_like(complexed(initial)) for axis_number in (1, 2, 3)]
    for iteration in range(ITERS):
        data_dual, data_back = lax.map(data_frame, (data_dual, measured, frame_weight, image_bar))
        image_complex = complexed(image_bar)
        time_dual = time_dual + SIGMA * jnp.fft.fft(image_complex, axis=0, norm='ortho')
        time_dual = time_dual / jnp.maximum(1.0, jnp.sqrt(squared(time_dual)) / limit_time)
        time_back = realed(jnp.fft.ifft(time_dual, axis=0, norm='ortho'))
        space_dual = [space_dual[index] + SIGMA * forward_diff(image_complex, axis_number) for index, axis_number in enumerate((1, 2, 3))]
        magnitude = jnp.sqrt(squared(space_dual[0]) + squared(space_dual[1]) + squared(space_dual[2]))
        factor = jnp.maximum(1.0, magnitude / limit_space)
        space_dual = [component / factor for component in space_dual]
        divergence = backward_diff(space_dual[0], 1) + backward_diff(space_dual[1], 2) + backward_diff(space_dual[2], 3)
        update = data_back + time_back + realed(divergence)
        updated = image - TAU * update
        image_bar = 2.0 * updated - image
        image = updated
    return image
```

```python
import math

import jax
import jax.numpy as jnp
import numpy as np
from jax import lax
from jax.experimental import pallas as pl
from jax.experimental.pallas import tpu as pltpu
from jax.sharding import PartitionSpec as P

ITERS = 2


TAU = 0.25
SIGMA = 0.25
LAM_TIME = 0.2
LAM_SPACE = 0.1
EPSILON = 1e-06
KEEP = 1.0 / (1.0 + SIGMA)
TAKE = SIGMA / (1.0 + SIGMA)
AXES = ("frame", "cuts")
STEP = 4
VMEM_BYTES = 56 * 1024 * 1024
BF16 = jnp.bfloat16
F32 = jnp.float32


def split_table(table):
    high = table.astype(np.float32).astype(BF16)
    low = (table - high.astype(np.float64)).astype(np.float32).astype(BF16)
    return high, low


def block_table(cosine, sine):
    return np.concatenate(
        [np.concatenate([cosine, sine], 1), np.concatenate([-sine, cosine], 1)], 0
    )


def line_tables(positions):
    half = positions // 2
    lines = np.arange(half)[:, None]
    tables = {}
    for name, places in (("even", 2 * np.arange(half)), ("odd", 2 * np.arange(half) + 1)):
        angles = 2.0 * math.pi / positions * (lines * places[None, :] % positions)
        back = block_table(np.cos(angles), np.sin(angles)) / math.sqrt(positions)
        for key, table in (("back_" + name, back), ("fore_" + name, back.T)):
            high, low = split_table(table)
            tables[key] = np.concatenate([high, high, low], 0)
    return tables


def time_tables(frames_all, frames_here):
    index = np.arange(frames_all)
    angles = 2.0 * math.pi / frames_all * (index[:, None] * index[None, :] % frames_all)
    fore = block_table(np.cos(angles), np.sin(angles)) / math.sqrt(frames_all)
    rows = np.concatenate([np.arange(frames_here), frames_all + np.arange(frames_here)])
    back = fore.T[rows]
    out = []
    for table in (fore, back):
        high, low = split_table(table)
        out.append(np.concatenate([high, high, low], 1))
    return out


def parting_table(positions):
    table = np.zeros((positions, positions), np.float32)
    half = positions // 2
    table[2 * np.arange(half), np.arange(half)] = 1.0
    table[2 * np.arange(half) + 1, half + np.arange(half)] = 1.0
    return table


def parted(value):
    high = value.astype(BF16)
    return high, (value - high.astype(F32)).astype(BF16)


def product(value, table):
    high, low = parted(value)
    return jnp.dot(
        jnp.concatenate([high, low, high], -1), table, preferred_element_type=F32
    )


def left_product(table, value):
    high, low = parted(value)
    return jnp.dot(
        table, jnp.concatenate([high, low, high], 0), preferred_element_type=F32
    )


def moved(value, table):
    first = value.astype(BF16)
    rest = value - first.astype(F32)
    second = rest.astype(BF16)
    third = (rest - second.astype(F32)).astype(BF16)
    return sum(
        jnp.dot(piece, table, preferred_element_type=F32) for piece in (first, second, third)
    )


def quarters(value):
    size = value.shape[-1] // 4
    return [value[..., index * size : (index + 1) * size] for index in range(4)]


def cat(*pieces):
    return jnp.concatenate(pieces, -1)


def combine_coils(coil_fields, maps):
    re, im = coil_fields[..., :128], coil_fields[..., 128:]
    map_re, map_im = maps[..., :128], maps[..., 128:]
    return cat(
        jnp.sum(map_re * re + map_im * im, axis=0), jnp.sum(map_re * im - map_im * re, axis=0)
    )


def initial_kernel(
    measured_ref, maps_ref, sampling_ref, even_ref, odd_ref, part_ref,
    image_ref, image_x_ref, energy_ref, parted_ref, total_ref,
):
    step = pl.program_id(0)
    frames = measured_ref.shape[0]
    coils, readout, doubled = maps_ref.shape[1:]
    half, quarter = doubled // 2, doubled // 4
    rows = coils * readout

    @pl.when(step == 0)
    def _():
        maps = maps_ref[0].reshape(rows, doubled)
        re = moved(maps[:, :half], part_ref[...])
        im = moved(maps[:, half:], part_ref[...])
        parted_ref[...] = cat(
            re[:, :quarter], im[:, :quarter], re[:, quarter:], im[:, quarter:]
        ).reshape(coils, readout, doubled)
        total_ref[...] = jnp.zeros_like(total_ref)

    evens, odds = [], []
    for index in range(frames):
        data = measured_ref[index, 0].reshape(rows, doubled)
        weight = sampling_ref[pl.ds(step * frames + index, 1), :].astype(F32)
        low, high = weight[:, :quarter], weight[:, quarter:]
        re_low, re_high, im_low, im_high = quarters(data)
        re_low, re_high = re_low * low, re_high * high
        im_low, im_high = im_low * low, im_high * high
        evens.append(cat(re_low + re_high, im_low + im_high))
        odds.append(cat(re_low - re_high, im_low - im_high))
    evens = product(jnp.concatenate(evens, 0), even_ref[...])
    odds = product(jnp.concatenate(odds, 0), odd_ref[...])
    evens = evens.reshape(frames, coils, readout, half)
    odds = odds.reshape(frames, coils, readout, half)
    energy = total_ref[...]
    for index in range(frames):
        image = cat(
            combine_coils(evens[index], parted_ref[:, :, :half]),
            combine_coils(odds[index], parted_ref[:, :, half:]),
        )
        image_ref[step * frames + index] = image
        energy = energy + sum(piece * piece for piece in quarters(image))
    total_ref[...] = energy

    @pl.when(step == pl.num_programs(0) - 1)
    def _():
        energy_ref[...] = jnp.broadcast_to(jnp.sum(total_ref[...]), energy_ref.shape)
        image_x_ref[...] = jnp.swapaxes(image_ref[...], 0, 1)


def normal_kernel(
    image_ref, maps_ref, sampling_ref, fore_even_ref, fore_odd_ref, even_ref, odd_ref,
    out_ref,
):
    step = pl.program_id(0)
    frames = image_ref.shape[0]
    coils, readout, doubled = maps_ref.shape
    half, quarter = doubled // 2, doubled // 4
    rows = coils * readout

    def lines(offset, table_ref):
        pieces = []
        for index in range(frames):
            re = image_ref[index, :, offset : offset + quarter][None]
            im = image_ref[index, :, offset + quarter : offset + half][None]
            map_re = maps_ref[:, :, offset : offset + quarter]
            map_im = maps_ref[:, :, offset + quarter : offset + half]
            pieces.append(
                cat(map_re * re - map_im * im, map_re * im + map_im * re).reshape(rows, half)
            )
        return product(jnp.concatenate(pieces, 0), table_ref[...])

    from_even = lines(0, fore_even_ref)
    from_odd = lines(half, fore_odd_ref)
    low = from_even + from_odd
    high = from_even - from_odd
    evens, odds = [], []
    for index in range(frames):
        weight = sampling_ref[pl.ds(step * frames + index, 1), :].astype(F32)
        weight_low = cat(weight[:, :quarter], weight[:, :quarter])
        weight_high = cat(weight[:, quarter:], weight[:, quarter:])
        kept_low = low[index * rows : (index + 1) * rows] * weight_low
        kept_high = high[index * rows : (index + 1) * rows] * weight_high
        evens.append(kept_low + kept_high)
        odds.append(kept_low - kept_high)
    evens = product(jnp.concatenate(evens, 0), even_ref[...])
    odds = product(jnp.concatenate(odds, 0), odd_ref[...])
    evens = evens.reshape(frames, coils, readout, half)
    odds = odds.reshape(frames, coils, readout, half)
    for index in range(frames):
        out_ref[index] = cat(
            combine_coils(evens[index], maps_ref[:, :, :half]),
            combine_coils(odds[index], maps_ref[:, :, half:]),
        )


def frequencies(blocks, x, table):
    parts = [quarters(block[x]) for block in blocks]
    re = jnp.concatenate([cat(part[0], part[2]) for part in parts], 0)
    im = jnp.concatenate([cat(part[1], part[3]) for part in parts], 0)
    return left_product(table, jnp.concatenate([re, im], 0))


def frequency_kernel(own_ref, one_ref, two_ref, three_ref, table_ref, out_ref):
    for x in range(own_ref.shape[0]):
        out_ref[x] = frequencies((own_ref, one_ref, two_ref, three_ref), x, table_ref[...])


def level(energy_ref, cells):
    total = jnp.sum(energy_ref[...], axis=0, keepdims=True)
    return jnp.sqrt(total / cells + EPSILON)


def clip_time(dual, limit):
    size = dual.shape[0] // 2
    re, im = dual[:size], dual[size:]
    scale = jnp.minimum(1.0, limit * lax.rsqrt(re * re + im * im))
    return jnp.concatenate([re * scale, im * scale], 0)


def frames_of(dual, table):
    field = left_product(table, dual)
    size, half = field.shape[0] // 2, field.shape[1] // 2
    re, im = field[:size], field[size:]
    return cat(re[:, :half], im[:, :half], re[:, half:], im[:, half:])


def later_lines(field):
    re_even, im_even, re_odd, im_odd = quarters(field)
    size = re_even.shape[-1]
    last = lax.broadcasted_iota(jnp.int32, re_even.shape, 1) == size - 1

    def rolled(piece):
        return jnp.where(last, 0.0, pltpu.roll(piece, size - 1, 1))

    return cat(re_odd, im_odd, rolled(re_even), rolled(im_even))


def earlier_lines(field):
    re_even, im_even, re_odd, im_odd = quarters(field)
    first = lax.broadcasted_iota(jnp.int32, re_even.shape, 1) == 0

    def rolled(piece):
        return jnp.where(first, 0.0, pltpu.roll(piece, 1, 1))

    return cat(rolled(re_odd), rolled(im_odd), re_even, im_even)


def clip_space(components, limit):
    re_even, im_even, re_odd, im_odd = (
        sum(piece * piece for piece in pieces)
        for pieces in zip(*(quarters(component) for component in components))
    )
    even = jnp.minimum(1.0, limit * lax.rsqrt(re_even + im_even))
    odd = jnp.minimum(1.0, limit * lax.rsqrt(re_odd + im_odd))
    scale = cat(even, even, odd, odd)
    return [component * scale for component in components]


def space_step(field, above, x, old, limit):
    readout = field.shape[0]
    here = field[x]
    further = field[x + 1] if x + 1 < readout else jnp.zeros_like(here)
    increments = (above[x] - here, further - here, later_lines(here) - here)
    if old is None:
        duals = [SIGMA * increment for increment in increments]
    else:
        duals = [
            old[index, x] + SIGMA * increment for index, increment in enumerate(increments)
        ]
    return clip_space(duals, limit)


def space_part(own, above, below, x, rows_before, has_below, old, old_below, limit):
    duals = space_step(own, above, x, old, limit)
    duals_below = space_step(below, own, x, old_below, limit)
    total = has_below * duals_below[0] - duals[0]
    total = total + (rows_before - duals[1])
    total = total + (earlier_lines(duals[2]) - duals[2])
    return total, duals, duals_below


def first_kernel(
    cells, energy_ref, flag_ref, own_ref, above_ref, below_ref, normal_ref, frequency_ref,
    table_ref,
    base_ref, bar_x_ref, bar_ref, time_ref, space_ref, space_below_ref,
):
    rms_level = level(energy_ref, cells)
    limit_time, limit_space = LAM_TIME * rms_level, LAM_SPACE * rms_level
    limit_wide = cat(limit_time, limit_time)
    has_below = flag_ref[0, 0]
    normal = jnp.swapaxes(normal_ref[...], 0, 1)
    rows_before = jnp.zeros(own_ref.shape[1:], F32)
    bars = []
    for x in range(own_ref.shape[0]):
        dual = clip_time(SIGMA * frequency_ref[x], limit_wide)
        time_ref[x] = dual
        total, duals, duals_below = space_part(
            own_ref, above_ref, below_ref, x, rows_before, has_below, None, None, limit_space
        )
        rows_before = duals[1]
        for index in range(3):
            space_ref[index, x] = duals[index]
            space_below_ref[index, x] = duals_below[index]
        initial = own_ref[x]
        data_part = TAKE * (normal[x] - initial)
        updated = initial - TAU * (data_part + frames_of(dual, table_ref[...]) + total)
        base_ref[x] = updated - TAU * (KEEP * data_part - TAKE * initial)
        bar = 2.0 * updated - initial
        bar_x_ref[x] = bar
        bars.append(bar)
    bar_ref[...] = jnp.swapaxes(jnp.stack(bars, 0), 0, 1)


def space_kernel(
    cells, energy_ref, flag_ref, own_ref, above_ref, below_ref, normal_ref, base_ref,
    space_ref, space_below_ref,
    out_ref,
):
    limit_space = LAM_SPACE * level(energy_ref, cells)
    has_below = flag_ref[0, 0]
    normal = jnp.swapaxes(normal_ref[...], 0, 1)
    rows_before = jnp.zeros(own_ref.shape[1:], F32)
    for x in range(own_ref.shape[0]):
        total, duals, _ = space_part(
            own_ref, above_ref, below_ref, x, rows_before, has_below,
            space_ref, space_below_ref, limit_space,
        )
        rows_before = duals[1]
        out_ref[x] = base_ref[x] - TAU * (TAKE * normal[x] + total)


def last_kernel(
    cells, energy_ref, own_ref, one_ref, two_ref, three_ref, time_ref, base_ref,
    fore_ref, back_ref, part_ref,
    out_ref,
):
    limit_time = LAM_TIME * level(energy_ref, cells)
    limit_wide = cat(limit_time, limit_time)
    blocks = (own_ref, one_ref, two_ref, three_ref)
    images = []
    for x in range(own_ref.shape[0]):
        dual = time_ref[x] + SIGMA * frequencies(blocks, x, fore_ref[...])
        field = frames_of(clip_time(dual, limit_wide), back_ref[...])
        images.append(base_ref[x] - TAU * field)
    count, size = len(images), images[0].shape[0]
    image = jnp.concatenate(images, 0)
    re_even, im_even, re_odd, im_odd = quarters(image)
    image = cat(
        moved(cat(re_even, re_odd), part_ref[...]), moved(cat(im_even, im_odd), part_ref[...])
    )
    out_ref[:, 0] = jnp.swapaxes(image.reshape(count, size, image.shape[-1]), 0, 1)


def params():
    return pltpu.CompilerParams(vmem_limit_bytes=VMEM_BYTES)


def cost(flops, moved_bytes):
    return pl.CostEstimate(flops=flops, bytes_accessed=moved_bytes, transcendentals=0)


def whole(array):
    return pl.BlockSpec(array.shape, lambda step: (0,) * array.ndim)


def struct(*shape):
    return jax.ShapeDtypeStruct(shape, F32)


def shards(measured, coil_maps, sampling):
    frames_here, slices_here, coils, readout, doubled = measured.shape
    positions = doubled // 2
    blocks = lax.axis_size("frame")
    slices_all = slices_here * lax.axis_size("cuts")
    frames_all = frames_here * blocks
    devices = blocks * lax.axis_size("cuts")
    cells = float(frames_all * slices_all * readout * positions)
    lines = {key: jnp.asarray(table) for key, table in line_tables(positions).items()}
    time_fore, time_back = (jnp.asarray(table) for table in time_tables(frames_all, frames_here))
    parting = parting_table(positions)
    part, unpart = jnp.asarray(parting, BF16), jnp.asarray(parting.T, BF16)
    plane = (readout, frames_here, doubled)
    turned = (frames_here, readout, doubled)
    rows = frames_here * coils * readout

    even, odd = lines["back_even"], lines["back_odd"]
    initial, initial_x, energy, maps = pl.pallas_call(
        initial_kernel,
        grid=(frames_here // STEP,),
        in_specs=[
            pl.BlockSpec((STEP,) + measured.shape[1:], lambda step: (step, 0, 0, 0, 0)),
            whole(coil_maps), whole(sampling), whole(even), whole(odd), whole(part),
        ],
        out_specs=[
            whole(struct(*turned)), whole(struct(*plane)), whole(struct(devices, 128)),
            whole(struct(coils, readout, doubled)),
        ],
        out_shape=[
            struct(*turned), struct(*plane), struct(devices, 128),
            struct(coils, readout, doubled),
        ],
        scratch_shapes=[pltpu.VMEM((readout, 128), F32)],
        compiler_params=params(),
        cost_estimate=cost(6 * rows * doubled * positions, measured.size * 4),
    )(measured, coil_maps, sampling, even, odd, part)

    energies = lax.all_to_all(energy, AXES, 0, 0, tiled=True)

    def normal(image):
        tables = [lines[key] for key in ("fore_even", "fore_odd", "back_even", "back_odd")]
        return pl.pallas_call(
            normal_kernel,
            grid=(frames_here // STEP,),
            in_specs=[
                pl.BlockSpec((STEP, readout, doubled), lambda step: (step, 0, 0)),
                whole(maps), whole(sampling),
            ] + [whole(table) for table in tables],
            out_specs=pl.BlockSpec((STEP, readout, doubled), lambda step: (step, 0, 0)),
            out_shape=struct(*turned),
            compiler_params=params(),
            cost_estimate=cost(12 * rows * doubled * positions, image.size * 8),
        )(image, maps, sampling, *tables)

    def gathered(image):
        others = [
            lax.ppermute(
                image, "frame", [((index + by) % blocks, index) for index in range(blocks)]
            )
            for by in range(1, blocks)
        ]
        return [image] + others

    def neighbours(image):
        count = lax.axis_size("cuts")
        above = lax.ppermute(image, "cuts", [(i + 1, i) for i in range(count - 1)])
        below = lax.ppermute(image, "cuts", [(i, i + 1) for i in range(count - 1)])
        return above, below

    flag = (lax.axis_index("cuts") > 0).astype(F32).reshape(1, 1)
    smem = pl.BlockSpec(memory_space=pltpu.SMEM)
    vmem = pl.BlockSpec(memory_space=pltpu.VMEM)

    def call(kernel, args, out_shape, flops):
        specs = [smem if arg is flag else vmem for arg in args]
        return pl.pallas_call(
            kernel,
            in_specs=specs,
            out_specs=jax.tree.map(lambda _: vmem, out_shape),
            out_shape=out_shape,
            compiler_params=params(),
            cost_estimate=cost(flops, sum(arg.size * 4 for arg in args)),
        )(*args)

    time_flops = 6 * (2 * frames_all) ** 2 * readout * positions
    all_blocks = gathered(initial_x)
    above, below = neighbours(initial_x)
    normal_initial = normal(initial)
    frequency_shape = struct(readout, 2 * frames_all, positions)
    frequency = call(frequency_kernel, all_blocks + [time_fore], frequency_shape, time_flops)
    duals_shape = struct(3, *plane)

    def first(*refs):
        first_kernel(cells, *refs)

    def space(*refs):
        space_kernel(cells, *refs)

    def last(*refs):
        last_kernel(cells, *refs)

    base, bar_x, bar, time_dual, space_dual, space_below = call(
        first,
        [energies, flag, initial_x, above, below, normal_initial, frequency, time_back],
        [struct(*plane), struct(*plane), struct(*turned), frequency_shape, duals_shape, duals_shape],
        time_flops // 4,
    )
    all_blocks = gathered(bar_x)
    above, below = neighbours(bar_x)
    normal_bar = normal(bar)
    base = call(
        space,
        [energies, flag, bar_x, above, below, normal_bar, base, space_dual, space_below],
        struct(*plane),
        1000000,
    )
    return call(
        last,
        [energies] + all_blocks + [time_dual, base, time_fore, time_back, unpart],
        struct(frames_here, slices_here, readout, doubled),
        time_flops,
    )


def solution(mesh):
    placed = (P("frame", "cuts", None, None, None), P("cuts", None, None, None), P("frame", None))
    return jax.shard_map(
        shards,
        mesh=mesh,
        in_specs=placed,
        out_specs=P("frame", "cuts", None, None),
        check_vma=False,
    )
```

```python
import math

import jax
import jax.numpy as jnp
import numpy as np
from jax import lax
from jax.experimental import pallas as pl
from jax.experimental.pallas import tpu as pltpu
from jax.sharding import PartitionSpec as P

ITERS = 2


TAU = 0.25
SIGMA = 0.25
LAM_TIME = 0.2
LAM_SPACE = 0.1
EPSILON = 1e-06
KEEP = 1.0 / (1.0 + SIGMA)
TAKE = SIGMA / (1.0 + SIGMA)
AXES = ("frame", "cuts")
STEP = 8
VMEM_BYTES = 24 * 1024 * 1024
BF16 = jnp.bfloat16
F32 = jnp.float32


def split_table(table):
    high = table.astype(np.float32).astype(BF16)
    low = (table - high.astype(np.float64)).astype(np.float32).astype(BF16)
    return high, low


def block_table(cosine, sine):
    return np.concatenate(
        [np.concatenate([cosine, sine], 1), np.concatenate([-sine, cosine], 1)], 0
    )


def line_tables(positions):
    half = positions // 2
    lines = np.arange(half)[:, None]
    backs = []
    for places in (2 * np.arange(half), 2 * np.arange(half) + 1):
        angles = 2.0 * math.pi / positions * (lines * places[None, :] % positions)
        back = block_table(np.cos(angles), np.sin(angles)) / math.sqrt(positions)
        backs.extend(split_table(back))
    return np.stack(backs, 0)


def time_tables(frames_all, frames_here):
    index = np.arange(frames_all)
    angles = 2.0 * math.pi / frames_all * (index[:, None] * index[None, :] % frames_all)
    fore = block_table(np.cos(angles), np.sin(angles)) / math.sqrt(frames_all)
    rows = np.concatenate([np.arange(frames_here), frames_all + np.arange(frames_here)])
    back = fore.T[rows]
    out = []
    for table in (fore, back):
        high, low = split_table(table)
        out.append(np.concatenate([high, high, low], 1))
    return out


def parting_table(positions):
    table = np.zeros((positions, positions), np.float32)
    half = positions // 2
    table[2 * np.arange(half), np.arange(half)] = 1.0
    table[2 * np.arange(half) + 1, half + np.arange(half)] = 1.0
    return table


def parted(value):
    high = value.astype(BF16)
    return high, (value - high.astype(F32)).astype(BF16)


def product(value, tables_ref, index):
    high, low = parted(value)
    table_high, table_low = tables_ref[index], tables_ref[index + 1]
    return jnp.dot(
        jnp.concatenate([high, low, high], -1),
        jnp.concatenate([table_high, table_high, table_low], 0),
        preferred_element_type=F32,
    )


def turned_product(value, tables_ref, index):
    high, low = parted(value)
    table_high, table_low = tables_ref[index], tables_ref[index + 1]
    return lax.dot_general(
        jnp.concatenate([high, low, high], -1),
        jnp.concatenate([table_high, table_high, table_low], -1),
        (((1,), (1,)), ((), ())),
        preferred_element_type=F32,
    )


def left_product(table, value):
    high, low = parted(value)
    return jnp.dot(
        table, jnp.concatenate([high, low, high], 0), preferred_element_type=F32
    )


def moved(value, table):
    first = value.astype(BF16)
    rest = value - first.astype(F32)
    second = rest.astype(BF16)
    third = (rest - second.astype(F32)).astype(BF16)
    return sum(
        jnp.dot(piece, table, preferred_element_type=F32) for piece in (first, second, third)
    )


def quarters(value):
    size = value.shape[-1] // 4
    return [value[..., index * size : (index + 1) * size] for index in range(4)]


def cat(*pieces):
    return jnp.concatenate(pieces, -1)


def combine_coils(coil_fields, maps):
    re, im = coil_fields[..., :128], coil_fields[..., 128:]
    map_re, map_im = maps[..., :128], maps[..., 128:]
    return cat(
        jnp.sum(map_re * re + map_im * im, axis=0), jnp.sum(map_re * im - map_im * re, axis=0)
    )


def initial_kernel(
    measured_hbm, maps_hbm, sampling_hbm, tables_hbm, part_hbm,
    image_ref, image_x_ref, energy_ref, parted_ref, tables_ref, sampling_ref,
    data_ref, maps_ref, part_ref, data_sem, sems,
):
    frames_here, coils, readout, doubled = data_ref.shape
    half, quarter = doubled // 2, doubled // 4
    rows = coils * readout
    groups = frames_here // STEP

    def load(group):
        frames = pl.ds(group * STEP, STEP)
        return pltpu.make_async_copy(
            measured_hbm.at[frames, 0], data_ref.at[frames], data_sem.at[group]
        )

    small = [
        pltpu.make_async_copy(maps_hbm.at[0], maps_ref, sems.at[0]),
        pltpu.make_async_copy(part_hbm, part_ref, sems.at[1]),
        pltpu.make_async_copy(sampling_hbm, sampling_ref, sems.at[2]),
        pltpu.make_async_copy(tables_hbm, tables_ref, sems.at[3]),
    ]
    for copy in small:
        copy.start()
    for group in range(groups):
        load(group).start()
    small[0].wait()
    small[1].wait()
    maps = maps_ref[...].reshape(rows, doubled)
    re = moved(maps[:, :half], part_ref[...])
    im = moved(maps[:, half:], part_ref[...])
    parted_ref[...] = cat(
        re[:, :quarter], im[:, :quarter], re[:, quarter:], im[:, quarter:]
    ).reshape(coils, readout, doubled)
    small[2].wait()
    small[3].wait()
    energy = jnp.zeros((readout, quarter), F32)
    for group in range(groups):
        load(group).wait()
        evens, odds = [], []
        for frame in range(group * STEP, (group + 1) * STEP):
            data = data_ref[frame].reshape(rows, doubled)
            weight = sampling_ref[frame : frame + 1, :].astype(F32)
            low, high = weight[:, :quarter], weight[:, quarter:]
            re_low, re_high, im_low, im_high = quarters(data)
            re_low, re_high = re_low * low, re_high * high
            im_low, im_high = im_low * low, im_high * high
            evens.append(cat(re_low + re_high, im_low + im_high))
            odds.append(cat(re_low - re_high, im_low - im_high))
        evens = product(jnp.concatenate(evens, 0), tables_ref, 0)
        odds = product(jnp.concatenate(odds, 0), tables_ref, 2)
        evens = evens.reshape(STEP, coils, readout, half)
        odds = odds.reshape(STEP, coils, readout, half)
        for index in range(STEP):
            image = cat(
                combine_coils(evens[index], parted_ref[:, :, :half]),
                combine_coils(odds[index], parted_ref[:, :, half:]),
            )
            image_ref[group * STEP + index] = image
            energy = energy + sum(piece * piece for piece in quarters(image))
    energy_ref[...] = jnp.broadcast_to(jnp.sum(energy), energy_ref.shape)
    image_x_ref[...] = jnp.swapaxes(image_ref[...], 0, 1)


def normal_kernel(image_ref, maps_ref, sampling_ref, tables_ref, out_ref):
    frames_here = image_ref.shape[0]
    coils, readout, doubled = maps_ref.shape
    half, quarter = doubled // 2, doubled // 4
    rows = coils * readout

    def lines(group, offset, table):
        pieces = []
        for index in range(STEP):
            frame = group * STEP + index
            re = image_ref[frame, :, offset : offset + quarter][None]
            im = image_ref[frame, :, offset + quarter : offset + half][None]
            map_re = maps_ref[:, :, offset : offset + quarter]
            map_im = maps_ref[:, :, offset + quarter : offset + half]
            pieces.append(
                cat(map_re * re - map_im * im, map_re * im + map_im * re).reshape(rows, half)
            )
        return turned_product(jnp.concatenate(pieces, 0), tables_ref, table)

    def step(group, carry):
        from_even = lines(group, 0, 0)
        from_odd = lines(group, half, 2)
        low = from_even + from_odd
        high = from_even - from_odd
        evens, odds = [], []
        for index in range(STEP):
            weight = sampling_ref[pl.ds(group * STEP + index, 1), :].astype(F32)
            weight_low = cat(weight[:, :quarter], weight[:, :quarter])
            weight_high = cat(weight[:, quarter:], weight[:, quarter:])
            kept_low = low[index * rows : (index + 1) * rows] * weight_low
            kept_high = high[index * rows : (index + 1) * rows] * weight_high
            evens.append(kept_low + kept_high)
            odds.append(kept_low - kept_high)
        evens = product(jnp.concatenate(evens, 0), tables_ref, 0)
        odds = product(jnp.concatenate(odds, 0), tables_ref, 2)
        evens = evens.reshape(STEP, coils, readout, half)
        odds = odds.reshape(STEP, coils, readout, half)
        for index in range(STEP):
            out_ref[group * STEP + index] = cat(
                combine_coils(evens[index], maps_ref[:, :, :half]),
                combine_coils(odds[index], maps_ref[:, :, half:]),
            )
        return carry

    lax.fori_loop(0, frames_here // STEP, step, 0)


def frequencies(blocks, x, table):
    parts = [quarters(block[x]) for block in blocks]
    re = jnp.concatenate([cat(part[0], part[2]) for part in parts], 0)
    im = jnp.concatenate([cat(part[1], part[3]) for part in parts], 0)
    return left_product(table, jnp.concatenate([re, im], 0))


def frequency_kernel(own_ref, one_ref, two_ref, three_ref, table_ref, out_ref):
    for x in range(own_ref.shape[0]):
        out_ref[x] = frequencies((own_ref, one_ref, two_ref, three_ref), x, table_ref[...])


def level(energy_ref, cells):
    total = jnp.sum(energy_ref[...], axis=0, keepdims=True)
    return jnp.sqrt(total / cells + EPSILON)


def clip_time(dual, limit):
    size = dual.shape[0] // 2
    re, im = dual[:size], dual[size:]
    scale = jnp.minimum(1.0, limit * lax.rsqrt(re * re + im * im))
    return jnp.concatenate([re * scale, im * scale], 0)


def frames_of(dual, table):
    field = left_product(table, dual)
    size, half = field.shape[0] // 2, field.shape[1] // 2
    re, im = field[:size], field[size:]
    return cat(re[:, :half], im[:, :half], re[:, half:], im[:, half:])


def later_lines(field):
    re_even, im_even, re_odd, im_odd = quarters(field)
    size = re_even.shape[-1]
    last = lax.broadcasted_iota(jnp.int32, re_even.shape, 1) == size - 1

    def rolled(piece):
        return jnp.where(last, 0.0, pltpu.roll(piece, size - 1, 1))

    return cat(re_odd, im_odd, rolled(re_even), rolled(im_even))


def earlier_lines(field):
    re_even, im_even, re_odd, im_odd = quarters(field)
    first = lax.broadcasted_iota(jnp.int32, re_even.shape, 1) == 0

    def rolled(piece):
        return jnp.where(first, 0.0, pltpu.roll(piece, 1, 1))

    return cat(rolled(re_odd), rolled(im_odd), re_even, im_even)


def clip_space(components, limit):
    re_even, im_even, re_odd, im_odd = (
        sum(piece * piece for piece in pieces)
        for pieces in zip(*(quarters(component) for component in components))
    )
    even = jnp.minimum(1.0, limit * lax.rsqrt(re_even + im_even))
    odd = jnp.minimum(1.0, limit * lax.rsqrt(re_odd + im_odd))
    scale = cat(even, even, odd, odd)
    return [component * scale for component in components]


def space_step(field, above, x, old, limit):
    readout = field.shape[0]
    here = field[x]
    further = field[x + 1] if x + 1 < readout else jnp.zeros_like(here)
    increments = (above[x] - here, further - here, later_lines(here) - here)
    if old is None:
        duals = [SIGMA * increment for increment in increments]
    else:
        duals = [
            old[index, x] + SIGMA * increment for index, increment in enumerate(increments)
        ]
    return clip_space(duals, limit)


def space_part(own, above, below, x, rows_before, has_below, old, old_below, limit):
    duals = space_step(own, above, x, old, limit)
    duals_below = space_step(below, own, x, old_below, limit)
    total = has_below * duals_below[0] - duals[0]
    total = total + (rows_before - duals[1])
    total = total + (earlier_lines(duals[2]) - duals[2])
    return total, duals, duals_below


def first_kernel(
    cells, energy_ref, own_ref, above_ref, below_ref, normal_ref, frequency_ref,
    table_ref,
    base_ref, bar_x_ref, bar_ref, time_ref, space_ref, space_below_ref,
):
    rms_level = level(energy_ref, cells)
    limit_time, limit_space = LAM_TIME * rms_level, LAM_SPACE * rms_level
    limit_wide = cat(limit_time, limit_time)
    has_below = (lax.axis_index("cuts") > 0).astype(F32)
    normal = jnp.swapaxes(normal_ref[...], 0, 1)
    rows_before = jnp.zeros(own_ref.shape[1:], F32)
    bars = []
    for x in range(own_ref.shape[0]):
        dual = clip_time(SIGMA * frequency_ref[x], limit_wide)
        time_ref[x] = dual
        total, duals, duals_below = space_part(
            own_ref, above_ref, below_ref, x, rows_before, has_below, None, None, limit_space
        )
        rows_before = duals[1]
        for index in range(3):
            space_ref[index, x] = duals[index]
            space_below_ref[index, x] = duals_below[index]
        initial = own_ref[x]
        data_part = TAKE * (normal[x] - initial)
        updated = initial - TAU * (data_part + frames_of(dual, table_ref[...]) + total)
        base_ref[x] = updated - TAU * (KEEP * data_part - TAKE * initial)
        bar = 2.0 * updated - initial
        bar_x_ref[x] = bar
        bars.append(bar)
    bar_ref[...] = jnp.swapaxes(jnp.stack(bars, 0), 0, 1)


def space_kernel(
    cells, energy_ref, own_ref, above_ref, below_ref, normal_ref, base_ref,
    space_ref, space_below_ref,
    out_ref,
):
    limit_space = LAM_SPACE * level(energy_ref, cells)
    has_below = (lax.axis_index("cuts") > 0).astype(F32)
    normal = jnp.swapaxes(normal_ref[...], 0, 1)
    rows_before = jnp.zeros(own_ref.shape[1:], F32)
    for x in range(own_ref.shape[0]):
        total, duals, _ = space_part(
            own_ref, above_ref, below_ref, x, rows_before, has_below,
            space_ref, space_below_ref, limit_space,
        )
        rows_before = duals[1]
        out_ref[x] = base_ref[x] - TAU * (TAKE * normal[x] + total)


def last_kernel(
    cells, energy_ref, own_ref, one_ref, two_ref, three_ref, time_ref, base_ref,
    fore_ref, back_ref, part_ref,
    out_ref,
):
    limit_time = LAM_TIME * level(energy_ref, cells)
    limit_wide = cat(limit_time, limit_time)
    blocks = (own_ref, one_ref, two_ref, three_ref)
    places = range(own_ref.shape[0])
    duals = [
        time_ref[x] + SIGMA * frequencies(blocks, x, fore_ref[...]) for x in places
    ]
    duals = [clip_time(dual, limit_wide) for dual in duals]
    images = [base_ref[x] - TAU * frames_of(duals[x], back_ref[...]) for x in places]
    count, size = len(images), images[0].shape[0]
    image = jnp.concatenate(images, 0)
    re_even, im_even, re_odd, im_odd = quarters(image)
    image = cat(
        moved(cat(re_even, re_odd), part_ref[...]), moved(cat(im_even, im_odd), part_ref[...])
    )
    out_ref[:, 0] = jnp.swapaxes(image.reshape(count, size, image.shape[-1]), 0, 1)


def params():
    return pltpu.CompilerParams(vmem_limit_bytes=VMEM_BYTES)


def cost(flops, moved_bytes):
    return pl.CostEstimate(flops=flops, bytes_accessed=moved_bytes, transcendentals=0)


def struct(*shape):
    return jax.ShapeDtypeStruct(shape, F32)


def shards(measured, coil_maps, sampling):
    frames_here, slices_here, coils, readout, doubled = measured.shape
    positions = doubled // 2
    blocks = lax.axis_size("frame")
    slices_all = slices_here * lax.axis_size("cuts")
    frames_all = frames_here * blocks
    devices = blocks * lax.axis_size("cuts")
    cells = float(frames_all * slices_all * readout * positions)
    tables = jnp.asarray(line_tables(positions))
    time_fore, time_back = (jnp.asarray(table) for table in time_tables(frames_all, frames_here))
    parting = parting_table(positions)
    part, unpart = jnp.asarray(parting, BF16), jnp.asarray(parting.T, BF16)
    plane = (readout, frames_here, doubled)
    turned = (frames_here, readout, doubled)
    rows = frames_here * coils * readout
    hbm = pl.BlockSpec(memory_space=pltpu.HBM)
    vmem = pl.BlockSpec(memory_space=pltpu.VMEM)

    initial, initial_x, energy, maps, tables, sampling = pl.pallas_call(
        initial_kernel,
        in_specs=[hbm] * 5,
        out_specs=[vmem] * 6,
        out_shape=[
            struct(*turned), struct(*plane), struct(devices, 128),
            pltpu.VMEM((coils, readout, doubled), F32),
            pltpu.VMEM(tables.shape, BF16),
            pltpu.VMEM(sampling.shape, jnp.int32),
        ],
        scratch_shapes=[
            pltpu.VMEM((frames_here, coils, readout, doubled), F32),
            pltpu.VMEM((coils, readout, doubled), F32),
            pltpu.VMEM(part.shape, BF16),
            pltpu.SemaphoreType.DMA((frames_here // STEP,)),
            pltpu.SemaphoreType.DMA((4,)),
        ],
        compiler_params=params(),
        cost_estimate=cost(6 * rows * doubled * positions, measured.size * 4),
    )(*(
        pltpu.with_memory_space_constraint(array, pltpu.HBM)
        for array in (measured, coil_maps, sampling, tables, part)
    ))

    energies = lax.all_to_all(energy, AXES, 0, 0, tiled=True)

    def normal(image):
        return pl.pallas_call(
            normal_kernel,
            in_specs=[vmem] * 4,
            out_specs=vmem,
            out_shape=struct(*turned),
            compiler_params=params(),
            cost_estimate=cost(12 * rows * doubled * positions, image.size * 8),
        )(image, *(
            pltpu.with_memory_space_constraint(array, pltpu.VMEM)
            for array in (maps, sampling, tables)
        ))

    def gathered(image):
        others = [
            lax.ppermute(
                image, "frame", [((index + by) % blocks, index) for index in range(blocks)]
            )
            for by in range(1, blocks)
        ]
        return [image] + others

    def neighbours(image):
        count = lax.axis_size("cuts")
        above = lax.ppermute(image, "cuts", [(i + 1, i) for i in range(count - 1)])
        below = lax.ppermute(image, "cuts", [(i, i + 1) for i in range(count - 1)])
        return above, below


    def call(kernel, args, out_shape, flops):
        return pl.pallas_call(
            kernel,
            in_specs=[vmem] * len(args),
            out_specs=jax.tree.map(lambda _: vmem, out_shape),
            out_shape=out_shape,
            compiler_params=params(),
            cost_estimate=cost(flops, sum(arg.size * 4 for arg in args)),
        )(*args)

    time_flops = 6 * (2 * frames_all) ** 2 * readout * positions
    all_blocks = gathered(initial_x)
    above, below = neighbours(initial_x)
    normal_initial = normal(initial)
    frequency_shape = struct(readout, 2 * frames_all, positions)
    frequency = call(frequency_kernel, all_blocks + [time_fore], frequency_shape, time_flops)
    duals_shape = struct(3, *plane)

    def first(*refs):
        first_kernel(cells, *refs)

    def space(*refs):
        space_kernel(cells, *refs)

    def last(*refs):
        last_kernel(cells, *refs)

    base, bar_x, bar, time_dual, space_dual, space_below = call(
        first,
        [energies, initial_x, above, below, normal_initial, frequency, time_back],
        [struct(*plane), struct(*plane), struct(*turned), frequency_shape, duals_shape, duals_shape],
        time_flops // 4,
    )
    all_blocks = gathered(bar_x)
    above, below = neighbours(bar_x)
    normal_bar = normal(bar)
    base = call(
        space,
        [energies, bar_x, above, below, normal_bar, base, space_dual, space_below],
        struct(*plane),
        1000000,
    )
    return call(
        last,
        [energies] + all_blocks + [time_dual, base, time_fore, time_back, unpart],
        struct(frames_here, slices_here, readout, doubled),
        time_flops,
    )


def solution(mesh):
    placed = (P("frame", "cuts", None, None, None), P("cuts", None, None, None), P("frame", None))
    return jax.shard_map(
        shards,
        mesh=mesh,
        in_specs=placed,
        out_specs=P("frame", "cuts", None, None),
        check_vma=False,
    )
```

```python
import math

import jax
import jax.numpy as jnp
import numpy as np
from jax import lax
from jax.experimental import pallas as pl
from jax.experimental.pallas import tpu as pltpu
from jax.sharding import PartitionSpec as P

ITERS = 2


TAU = 0.25
SIGMA = 0.25
LAM_TIME = 0.2
LAM_SPACE = 0.1
EPSILON = 1e-06
KEEP = 1.0 / (1.0 + SIGMA)
TAKE = SIGMA / (1.0 + SIGMA)
AXES = ("frame", "cuts")
STEP = 8
VMEM_BYTES = 24 * 1024 * 1024
BF16 = jnp.bfloat16
F32 = jnp.float32


def split_table(table):
    high = table.astype(np.float32).astype(BF16)
    low = (table - high.astype(np.float64)).astype(np.float32).astype(BF16)
    return high, low


def block_table(cosine, sine):
    return np.concatenate(
        [np.concatenate([cosine, sine], 1), np.concatenate([-sine, cosine], 1)], 0
    )


def line_tables(positions):
    half = positions // 2
    lines = np.arange(half)[:, None]
    backs = []
    for places in (2 * np.arange(half), 2 * np.arange(half) + 1):
        angles = 2.0 * math.pi / positions * (lines * places[None, :] % positions)
        back = block_table(np.cos(angles), np.sin(angles)) / math.sqrt(positions)
        backs.extend(split_table(back))
    return np.stack(backs, 0)


def time_tables(frames_all, frames_here):
    index = np.arange(frames_all)
    angles = 2.0 * math.pi / frames_all * (index[:, None] * index[None, :] % frames_all)
    fore = block_table(np.cos(angles), np.sin(angles)) / math.sqrt(frames_all)
    rows = np.concatenate([np.arange(frames_here), frames_all + np.arange(frames_here)])
    back = fore.T[rows]
    out = []
    for table in (fore, back):
        high, low = split_table(table)
        out.append(np.concatenate([high, high, low], 1))
    return out


def parting_table(positions):
    table = np.zeros((positions, positions), np.float32)
    half = positions // 2
    table[2 * np.arange(half), np.arange(half)] = 1.0
    table[2 * np.arange(half) + 1, half + np.arange(half)] = 1.0
    return table


def parted(value):
    high = value.astype(BF16)
    return high, (value - high.astype(F32)).astype(BF16)


def product(value, tables_ref, index):
    high, low = parted(value)
    table_high, table_low = tables_ref[index], tables_ref[index + 1]
    return jnp.dot(
        jnp.concatenate([high, low, high], -1),
        jnp.concatenate([table_high, table_high, table_low], 0),
        preferred_element_type=F32,
    )


def turned_product(value, tables_ref, index):
    high, low = parted(value)
    table_high, table_low = tables_ref[index], tables_ref[index + 1]
    return lax.dot_general(
        jnp.concatenate([high, low, high], -1),
        jnp.concatenate([table_high, table_high, table_low], -1),
        (((1,), (1,)), ((), ())),
        preferred_element_type=F32,
    )


def left_product(table, value):
    high, low = parted(value)
    return jnp.dot(
        table, jnp.concatenate([high, low, high], 0), preferred_element_type=F32
    )


def moved(value, table):
    first = value.astype(BF16)
    rest = value - first.astype(F32)
    second = rest.astype(BF16)
    third = (rest - second.astype(F32)).astype(BF16)
    return sum(
        jnp.dot(piece, table, preferred_element_type=F32) for piece in (first, second, third)
    )


def quarters(value):
    size = value.shape[-1] // 4
    return [value[..., index * size : (index + 1) * size] for index in range(4)]


def cat(*pieces):
    return jnp.concatenate(pieces, -1)


def combine_coils(coil_fields, maps):
    re, im = coil_fields[..., :128], coil_fields[..., 128:]
    map_re, map_im = maps[..., :128], maps[..., 128:]
    return cat(
        jnp.sum(map_re * re + map_im * im, axis=0), jnp.sum(map_re * im - map_im * re, axis=0)
    )


def initial_kernel(
    measured_hbm, maps_hbm, sampling_hbm, tables_hbm, part_hbm,
    image_ref, image_x_ref, energy_ref, parted_ref, tables_ref, sampling_ref,
    data_ref, maps_ref, part_ref, data_sem, sems,
):
    frames_here, coils, readout, doubled = data_ref.shape
    half, quarter = doubled // 2, doubled // 4
    rows = coils * readout
    groups = frames_here // STEP

    def load(group):
        frames = pl.ds(group * STEP, STEP)
        return pltpu.make_async_copy(
            measured_hbm.at[frames, 0], data_ref.at[frames], data_sem.at[group]
        )

    small = [
        pltpu.make_async_copy(maps_hbm.at[0], maps_ref, sems.at[0]),
        pltpu.make_async_copy(part_hbm, part_ref, sems.at[1]),
        pltpu.make_async_copy(sampling_hbm, sampling_ref, sems.at[2]),
        pltpu.make_async_copy(tables_hbm, tables_ref, sems.at[3]),
    ]
    for copy in small:
        copy.start()
    for group in range(groups):
        load(group).start()
    small[0].wait()
    small[1].wait()
    maps = maps_ref[...].reshape(rows, doubled)
    re = moved(maps[:, :half], part_ref[...])
    im = moved(maps[:, half:], part_ref[...])
    parted_ref[...] = cat(
        re[:, :quarter], im[:, :quarter], re[:, quarter:], im[:, quarter:]
    ).reshape(coils, readout, doubled)
    small[2].wait()
    small[3].wait()
    energy = jnp.zeros((readout, quarter), F32)
    for group in range(groups):
        load(group).wait()
        evens, odds = [], []
        for frame in range(group * STEP, (group + 1) * STEP):
            data = data_ref[frame].reshape(rows, doubled)
            weight = sampling_ref[frame : frame + 1, :].astype(F32)
            low, high = weight[:, :quarter], weight[:, quarter:]
            re_low, re_high, im_low, im_high = quarters(data)
            re_low, re_high = re_low * low, re_high * high
            im_low, im_high = im_low * low, im_high * high
            evens.append(cat(re_low + re_high, im_low + im_high))
            odds.append(cat(re_low - re_high, im_low - im_high))
        evens = product(jnp.concatenate(evens, 0), tables_ref, 0)
        odds = product(jnp.concatenate(odds, 0), tables_ref, 2)
        evens = evens.reshape(STEP, coils, readout, half)
        odds = odds.reshape(STEP, coils, readout, half)
        for index in range(STEP):
            image = cat(
                combine_coils(evens[index], parted_ref[:, :, :half]),
                combine_coils(odds[index], parted_ref[:, :, half:]),
            )
            image_ref[group * STEP + index] = image
            energy = energy + sum(piece * piece for piece in quarters(image))
    energy_ref[...] = jnp.broadcast_to(jnp.sum(energy), energy_ref.shape)
    image_x_ref[...] = jnp.swapaxes(image_ref[...], 0, 1)


def normal_kernel(image_ref, maps_ref, sampling_ref, tables_ref, out_ref):
    frames_here = image_ref.shape[0]
    coils, readout, doubled = maps_ref.shape
    half, quarter = doubled // 2, doubled // 4
    rows = coils * readout

    def lines(group, offset, table):
        pieces = []
        for index in range(STEP):
            frame = group * STEP + index
            re = image_ref[frame, :, offset : offset + quarter][None]
            im = image_ref[frame, :, offset + quarter : offset + half][None]
            map_re = maps_ref[:, :, offset : offset + quarter]
            map_im = maps_ref[:, :, offset + quarter : offset + half]
            pieces.append(
                cat(map_re * re - map_im * im, map_re * im + map_im * re).reshape(rows, half)
            )
        return turned_product(jnp.concatenate(pieces, 0), tables_ref, table)

    def step(group, carry):
        from_even = lines(group, 0, 0)
        from_odd = lines(group, half, 2)
        low = from_even + from_odd
        high = from_even - from_odd
        evens, odds = [], []
        for index in range(STEP):
            weight = sampling_ref[pl.ds(group * STEP + index, 1), :].astype(F32)
            weight_low = cat(weight[:, :quarter], weight[:, :quarter])
            weight_high = cat(weight[:, quarter:], weight[:, quarter:])
            kept_low = low[index * rows : (index + 1) * rows] * weight_low
            kept_high = high[index * rows : (index + 1) * rows] * weight_high
            evens.append(kept_low + kept_high)
            odds.append(kept_low - kept_high)
        evens = product(jnp.concatenate(evens, 0), tables_ref, 0)
        odds = product(jnp.concatenate(odds, 0), tables_ref, 2)
        evens = evens.reshape(STEP, coils, readout, half)
        odds = odds.reshape(STEP, coils, readout, half)
        for index in range(STEP):
            out_ref[group * STEP + index] = cat(
                combine_coils(evens[index], maps_ref[:, :, :half]),
                combine_coils(odds[index], maps_ref[:, :, half:]),
            )
        return carry

    lax.fori_loop(0, frames_here // STEP, step, 0)


def frequencies(blocks, x, table):
    parts = [quarters(block[x]) for block in blocks]
    re = jnp.concatenate([cat(part[0], part[2]) for part in parts], 0)
    im = jnp.concatenate([cat(part[1], part[3]) for part in parts], 0)
    return left_product(table, jnp.concatenate([re, im], 0))


def level(energy_ref, cells):
    total = jnp.sum(energy_ref[...], axis=0, keepdims=True)
    return jnp.sqrt(total / cells + EPSILON)


def clip_time(dual, limit):
    size = dual.shape[0] // 2
    re, im = dual[:size], dual[size:]
    scale = jnp.minimum(1.0, limit * lax.rsqrt(re * re + im * im))
    return jnp.concatenate([re * scale, im * scale], 0)


def frames_of(dual, table):
    field = left_product(table, dual)
    size, half = field.shape[0] // 2, field.shape[1] // 2
    re, im = field[:size], field[size:]
    return cat(re[:, :half], im[:, :half], re[:, half:], im[:, half:])


def later_lines(field):
    re_even, im_even, re_odd, im_odd = quarters(field)
    size = re_even.shape[-1]
    last = lax.broadcasted_iota(jnp.int32, re_even.shape, 1) == size - 1

    def rolled(piece):
        return jnp.where(last, 0.0, pltpu.roll(piece, size - 1, 1))

    return cat(re_odd, im_odd, rolled(re_even), rolled(im_even))


def earlier_lines(field):
    re_even, im_even, re_odd, im_odd = quarters(field)
    first = lax.broadcasted_iota(jnp.int32, re_even.shape, 1) == 0

    def rolled(piece):
        return jnp.where(first, 0.0, pltpu.roll(piece, 1, 1))

    return cat(rolled(re_odd), rolled(im_odd), re_even, im_even)


def clip_space(components, limit):
    re_even, im_even, re_odd, im_odd = (
        sum(piece * piece for piece in pieces)
        for pieces in zip(*(quarters(component) for component in components))
    )
    even = jnp.minimum(1.0, limit * lax.rsqrt(re_even + im_even))
    odd = jnp.minimum(1.0, limit * lax.rsqrt(re_odd + im_odd))
    scale = cat(even, even, odd, odd)
    return [component * scale for component in components]


def space_step(field, above, x, old, limit):
    readout = field.shape[0]
    here = field[x]
    further = field[x + 1] if x + 1 < readout else jnp.zeros_like(here)
    increments = (above[x] - here, further - here, later_lines(here) - here)
    if old is None:
        duals = [SIGMA * increment for increment in increments]
    else:
        duals = [
            old[index, x] + SIGMA * increment for index, increment in enumerate(increments)
        ]
    return clip_space(duals, limit)


def around(near_ref, far_ref):
    even = lax.axis_index("cuts") % 2 == 0
    near, far = near_ref[...], far_ref[...]
    return jnp.where(even, near, far), jnp.where(even, far, near)


def space_part(own, above, below, x, rows_before, has_below, old, old_below, limit):
    duals = space_step(own, above, x, old, limit)
    duals_below = space_step(below, own, x, old_below, limit)
    total = has_below * duals_below[0] - duals[0]
    total = total + (rows_before - duals[1])
    total = total + (earlier_lines(duals[2]) - duals[2])
    return total, duals, duals_below


def in_turn(own_ref, one_ref, two_ref, three_ref):
    even = lax.axis_index("frame") % 2 == 0
    one, three = one_ref[...], three_ref[...]
    return own_ref, jnp.where(even, one, three), two_ref, jnp.where(even, three, one)


def time_fields(blocks, level, old, fore_ref, back_ref, field_ref):
    places = range(field_ref.shape[0])
    limit = LAM_TIME * cat(level, level)
    duals = [SIGMA * frequencies(blocks, x, fore_ref[...]) for x in places]
    if old is not None:
        duals = [old[x] + dual for x, dual in zip(places, duals)]
    duals = [clip_time(dual, limit) for dual in duals]
    for x, dual in zip(places, duals):
        field_ref[x] = frames_of(dual, back_ref[...])
    return duals


def first_time_kernel(
    cells, energy_ref, own_ref, one_ref, two_ref, three_ref, fore_ref, back_ref,
    dual_ref, field_ref, level_ref,
):
    rms_level = level(energy_ref, cells)
    level_ref[...] = jnp.broadcast_to(rms_level, level_ref.shape)
    blocks = in_turn(own_ref, one_ref, two_ref, three_ref)
    duals = time_fields(blocks, rms_level, None, fore_ref, back_ref, field_ref)
    for x, dual in enumerate(duals):
        dual_ref[x] = dual


def last_time_kernel(
    level_ref, own_ref, one_ref, two_ref, three_ref, dual_ref, fore_ref, back_ref, field_ref
):
    blocks = in_turn(own_ref, one_ref, two_ref, three_ref)
    time_fields(blocks, level_ref[0:1, :], dual_ref, fore_ref, back_ref, field_ref)


def first_space_kernel(
    level_ref, own_ref, near_ref, far_ref, normal_ref, field_ref,
    base_ref, bar_x_ref, bar_ref, space_ref, space_below_ref,
):
    limit_space = LAM_SPACE * level_ref[0:1, :]
    has_below = (lax.axis_index("cuts") > 0).astype(F32)
    above, below = around(near_ref, far_ref)
    normal = jnp.swapaxes(normal_ref[...], 0, 1)
    rows_before = jnp.zeros(own_ref.shape[1:], F32)
    bars = []
    for x in range(own_ref.shape[0]):
        total, duals, duals_below = space_part(
            own_ref, above, below, x, rows_before, has_below, None, None, limit_space
        )
        rows_before = duals[1]
        for index in range(3):
            space_ref[index, x] = duals[index]
            space_below_ref[index, x] = duals_below[index]
        initial = own_ref[x]
        data_part = TAKE * (normal[x] - initial)
        updated = initial - TAU * (data_part + field_ref[x] + total)
        base_ref[x] = updated - TAU * (KEEP * data_part - TAKE * initial)
        bar = 2.0 * updated - initial
        bar_x_ref[x] = bar
        bars.append(bar)
    bar_ref[...] = jnp.swapaxes(jnp.stack(bars, 0), 0, 1)


def last_space_kernel(
    level_ref, own_ref, near_ref, far_ref, normal_ref, field_ref, base_ref,
    space_ref, space_below_ref, part_ref,
    out_ref,
):
    limit_space = LAM_SPACE * level_ref[0:1, :]
    has_below = (lax.axis_index("cuts") > 0).astype(F32)
    above, below = around(near_ref, far_ref)
    normal = jnp.swapaxes(normal_ref[...], 0, 1)
    rows_before = jnp.zeros(own_ref.shape[1:], F32)
    images = []
    for x in range(own_ref.shape[0]):
        total, duals, _ = space_part(
            own_ref, above, below, x, rows_before, has_below,
            space_ref, space_below_ref, limit_space,
        )
        rows_before = duals[1]
        images.append(base_ref[x] - TAU * (TAKE * normal[x] + field_ref[x] + total))
    image = jnp.concatenate(images, 0)
    re_even, im_even, re_odd, im_odd = quarters(image)
    image = cat(
        moved(cat(re_even, re_odd), part_ref[...]), moved(cat(im_even, im_odd), part_ref[...])
    )
    out_ref[:, 0] = jnp.swapaxes(image.reshape(own_ref.shape), 0, 1)


def stages(blocks, cuts):
    rows = 4 if cuts % 4 == 0 else 1
    index = np.arange(blocks * cuts).reshape(blocks * rows, cuts // rows)
    return index.T.tolist(), index.tolist()


def params():
    return pltpu.CompilerParams(vmem_limit_bytes=VMEM_BYTES)


def cost(flops, moved_bytes):
    return pl.CostEstimate(flops=flops, bytes_accessed=moved_bytes, transcendentals=0)


def struct(*shape):
    return jax.ShapeDtypeStruct(shape, F32)


def shards(measured, coil_maps, sampling):
    frames_here, slices_here, coils, readout, doubled = measured.shape
    positions = doubled // 2
    blocks = lax.axis_size("frame")
    slices_all = slices_here * lax.axis_size("cuts")
    frames_all = frames_here * blocks
    inner, outer = stages(blocks, lax.axis_size("cuts"))
    cells = float(frames_all * slices_all * readout * positions)
    tables = jnp.asarray(line_tables(positions))
    time_fore, time_back = (jnp.asarray(table) for table in time_tables(frames_all, frames_here))
    parting = parting_table(positions)
    part, unpart = jnp.asarray(parting, BF16), jnp.asarray(parting.T, BF16)
    plane = (readout, frames_here, doubled)
    turned = (frames_here, readout, doubled)
    rows = frames_here * coils * readout
    hbm = pl.BlockSpec(memory_space=pltpu.HBM)
    vmem = pl.BlockSpec(memory_space=pltpu.VMEM)

    initial, initial_x, energy, maps, tables, sampling = pl.pallas_call(
        initial_kernel,
        in_specs=[hbm] * 5,
        out_specs=[vmem] * 6,
        out_shape=[
            struct(*turned), struct(*plane), struct(len(inner[0]), 128),
            pltpu.VMEM((coils, readout, doubled), F32),
            pltpu.VMEM(tables.shape, BF16),
            pltpu.VMEM(sampling.shape, jnp.int32),
        ],
        scratch_shapes=[
            pltpu.VMEM((frames_here, coils, readout, doubled), F32),
            pltpu.VMEM((coils, readout, doubled), F32),
            pltpu.VMEM(part.shape, BF16),
            pltpu.SemaphoreType.DMA((frames_here // STEP,)),
            pltpu.SemaphoreType.DMA((4,)),
        ],
        compiler_params=params(),
        cost_estimate=cost(6 * rows * doubled * positions, measured.size * 4),
    )(*(
        pltpu.with_memory_space_constraint(array, pltpu.HBM)
        for array in (measured, coil_maps, sampling, tables, part)
    ))

    energies = lax.all_to_all(energy, AXES, 0, 0, tiled=True, axis_index_groups=inner)
    energies = jnp.broadcast_to(jnp.sum(energies, axis=0, keepdims=True), (len(outer[0]), 128))
    energies = lax.all_to_all(energies, AXES, 0, 0, tiled=True, axis_index_groups=outer)

    def normal(image):
        return pl.pallas_call(
            normal_kernel,
            in_specs=[vmem] * 4,
            out_specs=vmem,
            out_shape=struct(*turned),
            compiler_params=params(),
            cost_estimate=cost(12 * rows * doubled * positions, image.size * 8),
        )(image, *(
            pltpu.with_memory_space_constraint(array, pltpu.VMEM)
            for array in (maps, sampling, tables)
        ))

    def gathered(image):
        others = [
            lax.ppermute(image, "frame", [(index, index ^ by) for index in range(blocks)])
            for by in range(1, blocks)
        ]
        return [image] + others

    def neighbours(image):
        count = lax.axis_size("cuts")
        pairs = [[(i, i ^ 1) for i in range(count)], [(i, ((i + 1) ^ 1) - 1) for i in range(1, count - 1)]]
        return [lax.ppermute(image, "cuts", pair) for pair in pairs]


    def call(kernel, args, out_shape, flops):
        return pl.pallas_call(
            kernel,
            in_specs=[vmem] * len(args),
            out_specs=jax.tree.map(lambda _: vmem, out_shape),
            out_shape=out_shape,
            compiler_params=params(),
            cost_estimate=cost(flops, sum(arg.size * 4 for arg in args)),
        )(*args)

    time_flops = 7 * (2 * frames_all) ** 2 * readout * positions
    dual_shape = struct(readout, 2 * frames_all, positions)
    duals_shape = struct(3, *plane)

    def first_time(*refs):
        first_time_kernel(cells, *refs)

    all_blocks = gathered(initial_x)
    pair_near, pair_far = neighbours(initial_x)
    normal_initial = normal(initial)
    time_dual, field, rms_level = call(
        first_time,
        [energies] + all_blocks + [time_fore, time_back],
        [dual_shape, struct(*plane), struct(8, 128)],
        time_flops,
    )
    base, bar_x, bar, space_dual, space_below = call(
        first_space_kernel,
        [rms_level, initial_x, pair_near, pair_far, normal_initial, field],
        [struct(*plane), struct(*plane), struct(*turned), duals_shape, duals_shape],
        1000000,
    )
    all_blocks = gathered(bar_x)
    pair_near, pair_far = neighbours(bar_x)
    normal_bar = normal(bar)
    field = call(
        last_time_kernel,
        [rms_level] + all_blocks + [time_dual, time_fore, time_back],
        struct(*plane),
        time_flops,
    )
    return call(
        last_space_kernel,
        [rms_level, bar_x, pair_near, pair_far, normal_bar, field, base, space_dual, space_below, unpart],
        struct(frames_here, slices_here, readout, doubled),
        1000000,
    )


def solution(mesh):
    placed = (P("frame", "cuts", None, None, None), P("cuts", None, None, None), P("frame", None))
    return jax.shard_map(
        shards,
        mesh=mesh,
        in_specs=placed,
        out_specs=P("frame", "cuts", None, None),
        check_vma=False,
    )
```

```python
import math

import jax
import jax.numpy as jnp
import numpy as np
from jax import lax
from jax.experimental import pallas as pl
from jax.experimental.pallas import tpu as pltpu
from jax.sharding import PartitionSpec as P

ITERS = 2


TAU = 0.25
SIGMA = 0.25
LAM_TIME = 0.2
LAM_SPACE = 0.1
EPSILON = 1e-06
KEEP = 1.0 / (1.0 + SIGMA)
TAKE = SIGMA / (1.0 + SIGMA)
AXES = ("frame", "cuts")
GROUPS = (4, 6, 6)
NORMAL_STEP = 4
VMEM_BYTES = 24 * 1024 * 1024
BF16 = jnp.bfloat16
F32 = jnp.float32


def split_table(table):
    high = table.astype(np.float32).astype(BF16)
    low = (table - high.astype(np.float64)).astype(np.float32).astype(BF16)
    return high, low


def block_table(cosine, sine):
    return np.concatenate(
        [np.concatenate([cosine, sine], 1), np.concatenate([-sine, cosine], 1)], 0
    )


def line_tables(positions):
    half = positions // 2
    lines = np.arange(half)[:, None]
    backs = []
    for places in (2 * np.arange(half), 2 * np.arange(half) + 1):
        angles = 2.0 * math.pi / positions * (lines * places[None, :] % positions)
        back = block_table(np.cos(angles), np.sin(angles)) / math.sqrt(positions)
        backs.extend(split_table(back))
    return np.stack(backs, 0)


def time_tables(frames_all, frames_here):
    index = np.arange(frames_all)
    angles = 2.0 * math.pi / frames_all * (index[:, None] * index[None, :] % frames_all)
    fore = block_table(np.cos(angles), np.sin(angles)) / math.sqrt(frames_all)
    rows = np.concatenate([np.arange(frames_here), frames_all + np.arange(frames_here)])
    back = fore.T[rows]
    out = []
    for table in (fore, back):
        high, low = split_table(table)
        out.append(np.concatenate([high, high, low], 1))
    return out


def parting_table(positions):
    table = np.zeros((positions, positions), np.float32)
    half = positions // 2
    table[2 * np.arange(half), np.arange(half)] = 1.0
    table[2 * np.arange(half) + 1, half + np.arange(half)] = 1.0
    return table


def parted(value):
    high = value.astype(BF16)
    return high, (value - high.astype(F32)).astype(BF16)


def product(value, tables_ref, index):
    high, low = parted(value)
    table_high, table_low = tables_ref[index], tables_ref[index + 1]
    return jnp.dot(
        jnp.concatenate([high, low, high], -1),
        jnp.concatenate([table_high, table_high, table_low], 0),
        preferred_element_type=F32,
    )


def turned_product(value, tables_ref, index):
    high, low = parted(value)
    table_high, table_low = tables_ref[index], tables_ref[index + 1]
    return lax.dot_general(
        jnp.concatenate([high, low, high], -1),
        jnp.concatenate([table_high, table_high, table_low], -1),
        (((1,), (1,)), ((), ())),
        preferred_element_type=F32,
    )


def left_product(table, value):
    high, low = parted(value)
    return jnp.dot(
        table, jnp.concatenate([high, low, high], 0), preferred_element_type=F32
    )


def moved(value, table):
    first = value.astype(BF16)
    rest = value - first.astype(F32)
    second = rest.astype(BF16)
    third = (rest - second.astype(F32)).astype(BF16)
    return sum(
        jnp.dot(piece, table, preferred_element_type=F32) for piece in (first, second, third)
    )


def quarters(value):
    size = value.shape[-1] // 4
    return [value[..., index * size : (index + 1) * size] for index in range(4)]


def cat(*pieces):
    return jnp.concatenate(pieces, -1)


def combine_coils(coil_fields, maps):
    re, im = coil_fields[..., :128], coil_fields[..., 128:]
    map_re, map_im = maps[..., :128], maps[..., 128:]
    return cat(
        jnp.sum(map_re * re + map_im * im, axis=0), jnp.sum(map_re * im - map_im * re, axis=0)
    )


def initial_kernel(
    measured_hbm, maps_hbm, sampling_hbm, tables_hbm, part_hbm,
    image_ref, image_x_ref, energy_hbm, parted_ref, tables_ref, sampling_ref,
    data_ref, maps_ref, part_ref, energy_ref, data_sem, sems,
):
    frames_here, coils, readout, doubled = data_ref.shape
    half, quarter = doubled // 2, doubled // 4
    rows = coils * readout
    ends = [sum(GROUPS[:i]) for i in range(len(GROUPS) + 1)]
    groups = len(GROUPS)

    def load(group):
        frames = pl.ds(ends[group], GROUPS[group])
        return pltpu.make_async_copy(
            measured_hbm.at[frames, 0], data_ref.at[frames], data_sem.at[group]
        )

    small = [
        pltpu.make_async_copy(maps_hbm.at[0], maps_ref, sems.at[0]),
        pltpu.make_async_copy(part_hbm, part_ref, sems.at[1]),
        pltpu.make_async_copy(sampling_hbm, sampling_ref, sems.at[2]),
        pltpu.make_async_copy(tables_hbm, tables_ref, sems.at[3]),
    ]
    small[2].start()
    small[3].start()
    load(0).start()
    small[0].start()
    small[1].start()
    for group in range(1, groups):
        load(group).start()

    def part_maps():
        small[0].wait()
        small[1].wait()
        maps = maps_ref[...].reshape(rows, doubled)
        re = moved(maps[:, :half], part_ref[...])
        im = moved(maps[:, half:], part_ref[...])
        parted_ref[...] = cat(
            re[:, :quarter], im[:, :quarter], re[:, quarter:], im[:, quarter:]
        ).reshape(coils, readout, doubled)

    small[2].wait()
    small[3].wait()
    energy = jnp.zeros((readout, quarter), F32)
    for group in range(groups):
        load(group).wait()
        evens, odds = [], []
        count = GROUPS[group]
        for frame in range(ends[group], ends[group + 1]):
            data = data_ref[frame].reshape(rows, doubled)
            weight = sampling_ref[frame : frame + 1, :].astype(F32)
            low, high = weight[:, :quarter], weight[:, quarter:]
            re_low, re_high, im_low, im_high = quarters(data)
            re_low, re_high = re_low * low, re_high * high
            im_low, im_high = im_low * low, im_high * high
            evens.append(cat(re_low + re_high, im_low + im_high))
            odds.append(cat(re_low - re_high, im_low - im_high))
        evens = product(jnp.concatenate(evens, 0), tables_ref, 0)
        odds = product(jnp.concatenate(odds, 0), tables_ref, 2)
        evens = evens.reshape(count, coils, readout, half)
        odds = odds.reshape(count, coils, readout, half)
        if group == 0:
            part_maps()
        for index in range(count):
            image = cat(
                combine_coils(evens[index], parted_ref[:, :, :half]),
                combine_coils(odds[index], parted_ref[:, :, half:]),
            )
            image_ref[ends[group] + index] = image
            energy = energy + sum(piece * piece for piece in quarters(image))
    energy_ref[...] = jnp.broadcast_to(jnp.sum(energy), energy_ref.shape)
    send = pltpu.make_async_copy(energy_ref, energy_hbm, sems.at[4])
    send.start()
    image_x_ref[...] = jnp.swapaxes(image_ref[...], 0, 1)
    send.wait()


def normal_kernel(begin, image_ref, maps_ref, sampling_ref, tables_ref, *rest):
    out_ref = rest[-1]
    frames_here = out_ref.shape[0]
    coils, readout, doubled = maps_ref.shape
    half, quarter = doubled // 2, doubled // 4
    rows = coils * readout

    def lines(group, offset, table):
        pieces = []
        for index in range(NORMAL_STEP):
            frame = begin + group * NORMAL_STEP + index
            re = image_ref[frame, :, offset : offset + quarter][None]
            im = image_ref[frame, :, offset + quarter : offset + half][None]
            map_re = maps_ref[:, :, offset : offset + quarter]
            map_im = maps_ref[:, :, offset + quarter : offset + half]
            pieces.append(
                cat(map_re * re - map_im * im, map_re * im + map_im * re).reshape(rows, half)
            )
        return turned_product(jnp.concatenate(pieces, 0), tables_ref, table)

    def forth(group):
        from_even = lines(group, 0, 0)
        from_odd = lines(group, half, 2)
        low = from_even + from_odd
        high = from_even - from_odd
        evens, odds = [], []
        for index in range(NORMAL_STEP):
            frame = begin + group * NORMAL_STEP + index
            weight = sampling_ref[frame : frame + 1, :].astype(F32)
            weight_low = cat(weight[:, :quarter], weight[:, :quarter])
            weight_high = cat(weight[:, quarter:], weight[:, quarter:])
            kept_low = low[index * rows : (index + 1) * rows] * weight_low
            kept_high = high[index * rows : (index + 1) * rows] * weight_high
            evens.append(kept_low + kept_high)
            odds.append(kept_low - kept_high)
        return jnp.concatenate(evens, 0), jnp.concatenate(odds, 0)

    def back(group, evens, odds):
        evens = product(evens, tables_ref, 0).reshape(NORMAL_STEP, coils, readout, half)
        odds = product(odds, tables_ref, 2).reshape(NORMAL_STEP, coils, readout, half)
        for index in range(NORMAL_STEP):
            out_ref[group * NORMAL_STEP + index] = cat(
                combine_coils(evens[index], maps_ref[:, :, :half]),
                combine_coils(odds[index], maps_ref[:, :, half:]),
            )

    groups = frames_here // NORMAL_STEP
    held = forth(0)
    for group in range(groups):
        later = forth(group + 1) if group + 1 < groups else None
        back(group, *held)
        held = later


def frequencies(blocks, x, table):
    parts = [quarters(block[x]) for block in blocks]
    re = jnp.concatenate([cat(part[0], part[2]) for part in parts], 0)
    im = jnp.concatenate([cat(part[1], part[3]) for part in parts], 0)
    return left_product(table, jnp.concatenate([re, im], 0))


def level(energy_ref, cells):
    total = jnp.sum(energy_ref[...], axis=0, keepdims=True)
    return jnp.sqrt(total / cells + EPSILON)


def clip_time(dual, limit):
    size = dual.shape[0] // 2
    re, im = dual[:size], dual[size:]
    scale = jnp.minimum(1.0, limit * lax.rsqrt(re * re + im * im))
    return jnp.concatenate([re * scale, im * scale], 0)


def frames_of(dual, table):
    field = left_product(table, dual)
    size, half = field.shape[0] // 2, field.shape[1] // 2
    re, im = field[:size], field[size:]
    return cat(re[:, :half], im[:, :half], re[:, half:], im[:, half:])


def later_lines(field):
    re_even, im_even, re_odd, im_odd = quarters(field)
    size = re_even.shape[-1]
    last = lax.broadcasted_iota(jnp.int32, re_even.shape, 1) == size - 1

    def rolled(piece):
        return jnp.where(last, 0.0, pltpu.roll(piece, size - 1, 1))

    return cat(re_odd, im_odd, rolled(re_even), rolled(im_even))


def earlier_lines(field):
    re_even, im_even, re_odd, im_odd = quarters(field)
    first = lax.broadcasted_iota(jnp.int32, re_even.shape, 1) == 0

    def rolled(piece):
        return jnp.where(first, 0.0, pltpu.roll(piece, 1, 1))

    return cat(rolled(re_odd), rolled(im_odd), re_even, im_even)


def clip_space(components, limit):
    re_even, im_even, re_odd, im_odd = (
        sum(piece * piece for piece in pieces)
        for pieces in zip(*(quarters(component) for component in components))
    )
    even = jnp.minimum(1.0, limit * lax.rsqrt(re_even + im_even))
    odd = jnp.minimum(1.0, limit * lax.rsqrt(re_odd + im_odd))
    scale = cat(even, even, odd, odd)
    return [component * scale for component in components]


def space_step(field, above, x, old, limit):
    readout = field.shape[0]
    here = field[x]
    further = field[x + 1] if x + 1 < readout else jnp.zeros_like(here)
    increments = (above[x] - here, further - here, later_lines(here) - here)
    if old is None:
        duals = [SIGMA * increment for increment in increments]
    else:
        duals = [
            old[index, x] + SIGMA * increment for index, increment in enumerate(increments)
        ]
    return clip_space(duals, limit)


def around(near_ref, far_ref):
    even = lax.axis_index("cuts") % 2 == 0
    near, far = near_ref[...], far_ref[...]
    return jnp.where(even, near, far), jnp.where(even, far, near)


def space_part(own, above, below, x, rows_before, has_below, old, old_below, limit):
    duals = space_step(own, above, x, old, limit)
    duals_below = space_step(below, own, x, old_below, limit)
    total = has_below * duals_below[0] - duals[0]
    total = total + (rows_before - duals[1])
    total = total + (earlier_lines(duals[2]) - duals[2])
    return total, duals, duals_below


def in_turn(own_ref, one_ref, two_ref, three_ref):
    even = lax.axis_index("frame") % 2 == 0
    one, three = one_ref[...], three_ref[...]
    return own_ref, jnp.where(even, one, three), two_ref, jnp.where(even, three, one)


def time_duals(duals, level):
    limit = LAM_TIME * cat(level, level)
    return [clip_time(dual, limit) for dual in duals]


def summed_kernel(energy_ref, out_ref):
    out_ref[...] = jnp.broadcast_to(
        jnp.sum(energy_ref[...], axis=0, keepdims=True), out_ref.shape
    )


def frequency_kernel(own_ref, one_ref, two_ref, three_ref, fore_ref, out_ref):
    blocks = in_turn(own_ref, one_ref, two_ref, three_ref)
    for x in range(own_ref.shape[0]):
        out_ref[x] = SIGMA * frequencies(blocks, x, fore_ref[...])


def last_time_kernel(
    level_ref, own_ref, one_ref, two_ref, three_ref, dual_ref, fore_ref, back_ref, field_ref
):
    blocks = in_turn(own_ref, one_ref, two_ref, three_ref)
    places = range(field_ref.shape[0])
    duals = [dual_ref[x] + SIGMA * frequencies(blocks, x, fore_ref[...]) for x in places]
    duals = time_duals(duals, level_ref[0:1, :])
    for x, dual in enumerate(duals):
        field_ref[x] = frames_of(dual, back_ref[...])


def first_kernel(
    cells, energy_ref, own_ref, near_ref, far_ref, normal_ref, frequency_ref, back_ref,
    base_ref, bar_x_ref, bar_ref, dual_ref, level_ref, space_ref, space_below_ref,
):
    rms_level = level(energy_ref, cells)
    level_ref[...] = jnp.broadcast_to(rms_level, level_ref.shape)
    time = time_duals([frequency_ref[x] for x in range(frequency_ref.shape[0])], rms_level)
    for x, dual in enumerate(time):
        dual_ref[x] = dual
    fields = [frames_of(dual, back_ref[...]) for dual in time]
    limit_space = LAM_SPACE * rms_level
    has_below = (lax.axis_index("cuts") > 0).astype(F32)
    above, below = around(near_ref, far_ref)
    normal = jnp.swapaxes(normal_ref[...], 0, 1)
    rows_before = jnp.zeros(own_ref.shape[1:], F32)
    bars = []
    for x in range(own_ref.shape[0]):
        total, duals, duals_below = space_part(
            own_ref, above, below, x, rows_before, has_below, None, None, limit_space
        )
        rows_before = duals[1]
        for index in range(3):
            space_ref[index, x] = duals[index]
            space_below_ref[index, x] = duals_below[index]
        initial = own_ref[x]
        data_part = TAKE * (normal[x] - initial)
        updated = initial - TAU * (data_part + fields[x] + total)
        base_ref[x] = updated - TAU * (KEEP * data_part - TAKE * initial)
        bar = 2.0 * updated - initial
        bar_x_ref[x] = bar
        bars.append(bar)
    bar_ref[...] = jnp.swapaxes(jnp.stack(bars, 0), 0, 1)


def last_space_kernel(
    level_ref, own_ref, near_ref, far_ref, normal_ref, field_ref, base_ref,
    space_ref, space_below_ref, part_ref,
    out_ref,
):
    limit_space = LAM_SPACE * level_ref[0:1, :]
    has_below = (lax.axis_index("cuts") > 0).astype(F32)
    above, below = around(near_ref, far_ref)
    normal = jnp.swapaxes(normal_ref[...], 0, 1)
    rows_before = jnp.zeros(own_ref.shape[1:], F32)
    images = []
    for x in range(own_ref.shape[0]):
        total, duals, _ = space_part(
            own_ref, above, below, x, rows_before, has_below,
            space_ref, space_below_ref, limit_space,
        )
        rows_before = duals[1]
        images.append(base_ref[x] - TAU * (TAKE * normal[x] + field_ref[x] + total))
    image = jnp.concatenate(images, 0)
    re_even, im_even, re_odd, im_odd = quarters(image)
    image = cat(
        moved(cat(re_even, re_odd), part_ref[...]), moved(cat(im_even, im_odd), part_ref[...])
    )
    out_ref[:, 0] = jnp.swapaxes(image.reshape(own_ref.shape), 0, 1)


def stages(blocks, cuts):
    rows = 4 if cuts % 4 == 0 else 1
    index = np.arange(blocks * cuts).reshape(blocks * rows, cuts // rows)
    return index.T.tolist(), index.tolist()


def params():
    return pltpu.CompilerParams(vmem_limit_bytes=VMEM_BYTES)


def cost(flops, moved_bytes):
    return pl.CostEstimate(flops=flops, bytes_accessed=moved_bytes, transcendentals=0)


def struct(*shape):
    return jax.ShapeDtypeStruct(shape, F32)


def shards(measured, coil_maps, sampling):
    frames_here, slices_here, coils, readout, doubled = measured.shape
    positions = doubled // 2
    blocks = lax.axis_size("frame")
    slices_all = slices_here * lax.axis_size("cuts")
    frames_all = frames_here * blocks
    inner, outer = stages(blocks, lax.axis_size("cuts"))
    cells = float(frames_all * slices_all * readout * positions)
    tables = jnp.asarray(line_tables(positions))
    time_fore, time_back = (jnp.asarray(table) for table in time_tables(frames_all, frames_here))
    parting = parting_table(positions)
    part, unpart = jnp.asarray(parting, BF16), jnp.asarray(parting.T, BF16)
    plane = (readout, frames_here, doubled)
    turned = (frames_here, readout, doubled)
    rows = frames_here * coils * readout
    hbm = pl.BlockSpec(memory_space=pltpu.HBM)
    vmem = pl.BlockSpec(memory_space=pltpu.VMEM)

    initial, initial_x, energy, maps, tables, sampling = pl.pallas_call(
        initial_kernel,
        in_specs=[hbm] * 5,
        out_specs=[vmem] * 2 + [pl.BlockSpec(memory_space=pl.ANY)] + [vmem] * 3,
        out_shape=[
            struct(*turned), struct(*plane), struct(len(inner[0]), 128),
            pltpu.VMEM((coils, readout, doubled), F32),
            pltpu.VMEM(tables.shape, BF16),
            pltpu.VMEM(sampling.shape, jnp.int32),
        ],
        scratch_shapes=[
            pltpu.VMEM((frames_here, coils, readout, doubled), F32),
            pltpu.VMEM((coils, readout, doubled), F32),
            pltpu.VMEM(part.shape, BF16),
            pltpu.VMEM((len(inner[0]), 128), F32),
            pltpu.SemaphoreType.DMA((len(GROUPS),)),
            pltpu.SemaphoreType.DMA((5,)),
        ],
        compiler_params=params(),
        cost_estimate=cost(6 * rows * doubled * positions, measured.size * 4),
    )(*(
        pltpu.with_memory_space_constraint(array, pltpu.HBM)
        for array in (measured, coil_maps, sampling, tables, part)
    ))

    def normal(image, begin=0, count=frames_here, after=()):
        def kernel(*refs):
            normal_kernel(begin, *refs)

        return pl.pallas_call(
            kernel,
            in_specs=[vmem] * (4 + len(after)),
            out_specs=vmem,
            out_shape=struct(count, readout, doubled),
            compiler_params=params(),
            cost_estimate=cost(12 * rows * doubled * positions * count // frames_here, 1000000),
        )(image, *(
            pltpu.with_memory_space_constraint(array, pltpu.VMEM)
            for array in (maps, sampling, tables)
        ), *after)

    def swapped(image, by):
        return lax.ppermute(image, "frame", [(index, index ^ by) for index in range(blocks)])

    def gathered(image):
        return [image] + [swapped(image, by) for by in range(1, blocks)]

    def neighbours(image):
        count = lax.axis_size("cuts")
        pairs = [[(i, i ^ 1) for i in range(count)], [(i, ((i + 1) ^ 1) - 1) for i in range(1, count - 1)]]
        return [lax.ppermute(image, "cuts", pair) for pair in pairs]


    def call(kernel, args, out_shape, flops):
        return pl.pallas_call(
            kernel,
            in_specs=[vmem] * len(args),
            out_specs=jax.tree.map(lambda _: vmem, out_shape),
            out_shape=out_shape,
            compiler_params=params(),
            cost_estimate=cost(flops, sum(arg.size * 4 for arg in args)),
        )(*args)

    energies = lax.all_to_all(energy, AXES, 0, 0, tiled=True, axis_index_groups=inner)
    energies = call(summed_kernel, [energies], pltpu.VMEM((len(outer[0]), 128), F32), 1000)
    energies = lax.all_to_all(energies, AXES, 0, 0, tiled=True, axis_index_groups=outer)

    time_flops = 7 * (2 * frames_all) ** 2 * readout * positions
    dual_shape = struct(readout, 2 * frames_all, positions)
    duals_shape = struct(3, *plane)

    def first(*refs):
        first_kernel(cells, *refs)

    all_blocks = gathered(initial_x)
    pair_near, pair_far = neighbours(initial_x)
    normal_initial = normal(initial)
    frequency = call(frequency_kernel, all_blocks + [time_fore], dual_shape, time_flops // 2)
    base, bar_x, bar, time_dual, rms_level, space_dual, space_below = call(
        first,
        [energies, initial_x, pair_near, pair_far, normal_initial, frequency, time_back],
        [
            struct(*plane), struct(*plane), struct(*turned), dual_shape, struct(8, 128),
            duals_shape, duals_shape,
        ],
        time_flops // 2,
    )
    all_blocks = gathered(bar_x)
    pair_near, pair_far = neighbours(bar_x)
    normal_bar = normal(bar)
    field = call(
        last_time_kernel,
        [rms_level] + all_blocks + [time_dual, time_fore, time_back],
        struct(*plane),
        time_flops,
    )
    return call(
        last_space_kernel,
        [rms_level, bar_x, pair_near, pair_far, normal_bar, field, base, space_dual, space_below, unpart],
        struct(frames_here, slices_here, readout, doubled),
        1000000,
    )


def solution(mesh):
    placed = (P("frame", "cuts", None, None, None), P("cuts", None, None, None), P("frame", None))
    return jax.shard_map(
        shards,
        mesh=mesh,
        in_specs=placed,
        out_specs=P("frame", "cuts", None, None),
        check_vma=False,
    )
```

```python
import math

import jax
import jax.numpy as jnp
import numpy as np
from jax import lax
from jax.experimental import pallas as pl
from jax.experimental.pallas import tpu as pltpu
from jax.sharding import PartitionSpec as P

ITERS = 2


TAU = 0.25
SIGMA = 0.25
LAM_TIME = 0.2
LAM_SPACE = 0.1
EPSILON = 1e-06
KEEP = 1.0 / (1.0 + SIGMA)
TAKE = SIGMA / (1.0 + SIGMA)
AXES = ("frame", "cuts")
GROUPS = (4, 6, 6)
NORMAL_STEP = 4
VMEM_BYTES = 24 * 1024 * 1024
BF16 = jnp.bfloat16
F32 = jnp.float32


def split_table(table):
    high = table.astype(np.float32).astype(BF16)
    low = (table - high.astype(np.float64)).astype(np.float32).astype(BF16)
    return high, low


def block_table(cosine, sine):
    return np.concatenate(
        [np.concatenate([cosine, sine], 1), np.concatenate([-sine, cosine], 1)], 0
    )


def line_tables(positions):
    half = positions // 2
    lines = np.arange(half)[:, None]
    backs = []
    for places in (2 * np.arange(half), 2 * np.arange(half) + 1):
        angles = 2.0 * math.pi / positions * (lines * places[None, :] % positions)
        back = block_table(np.cos(angles), np.sin(angles)) / math.sqrt(positions)
        backs.extend(split_table(back))
    return np.stack(backs, 0)


def time_tables(frames_all, frames_here):
    index = np.arange(frames_all)
    angles = 2.0 * math.pi / frames_all * (index[:, None] * index[None, :] % frames_all)
    fore = block_table(np.cos(angles), np.sin(angles)) / math.sqrt(frames_all)
    rows = np.concatenate([np.arange(frames_here), frames_all + np.arange(frames_here)])
    out = []
    last = frames_all // frames_here - 1
    for table in (fore, fore.T[rows], fore[:, rows + frames_here], fore[:, rows + last * frames_here]):
        high, low = split_table(table)
        out.append(np.concatenate([high, high, low], 1))
    return out[0], out[1], np.stack(out[2:], 0)


def parting_table(positions):
    table = np.zeros((positions, positions), np.float32)
    half = positions // 2
    table[2 * np.arange(half), np.arange(half)] = 1.0
    table[2 * np.arange(half) + 1, half + np.arange(half)] = 1.0
    return table


def parted(value):
    high = value.astype(BF16)
    return high, (value - high.astype(F32)).astype(BF16)


def product(value, tables_ref, index):
    high, low = parted(value)
    table_high, table_low = tables_ref[index], tables_ref[index + 1]
    return jnp.dot(
        jnp.concatenate([high, low, high], -1),
        jnp.concatenate([table_high, table_high, table_low], 0),
        preferred_element_type=F32,
    )


def turned_product(value, tables_ref, index):
    high, low = parted(value)
    table_high, table_low = tables_ref[index], tables_ref[index + 1]
    return lax.dot_general(
        jnp.concatenate([high, low, high], -1),
        jnp.concatenate([table_high, table_high, table_low], -1),
        (((1,), (1,)), ((), ())),
        preferred_element_type=F32,
    )


def left_product(table, value):
    high, low = parted(value)
    return jnp.dot(
        table, jnp.concatenate([high, low, high], 0), preferred_element_type=F32
    )


def moved(value, table):
    first = value.astype(BF16)
    rest = value - first.astype(F32)
    second = rest.astype(BF16)
    third = (rest - second.astype(F32)).astype(BF16)
    return sum(
        jnp.dot(piece, table, preferred_element_type=F32) for piece in (first, second, third)
    )


def quarters(value):
    size = value.shape[-1] // 4
    return [value[..., index * size : (index + 1) * size] for index in range(4)]


def cat(*pieces):
    return jnp.concatenate(pieces, -1)


def combine_coils(coil_fields, maps):
    re, im = coil_fields[..., :128], coil_fields[..., 128:]
    map_re, map_im = maps[..., :128], maps[..., 128:]
    return cat(
        jnp.sum(map_re * re + map_im * im, axis=0), jnp.sum(map_re * im - map_im * re, axis=0)
    )


def initial_kernel(
    measured_hbm, maps_hbm, sampling_hbm, tables_hbm, part_hbm,
    image_ref, image_x_ref, energy_hbm, parted_ref, tables_ref, sampling_ref,
    data_ref, maps_ref, part_ref, energy_ref, data_sem, sems,
):
    frames_here, coils, readout, doubled = data_ref.shape
    half, quarter = doubled // 2, doubled // 4
    rows = coils * readout
    ends = [sum(GROUPS[:i]) for i in range(len(GROUPS) + 1)]
    groups = len(GROUPS)

    def load(group):
        frames = pl.ds(ends[group], GROUPS[group])
        return pltpu.make_async_copy(
            measured_hbm.at[frames, 0], data_ref.at[frames], data_sem.at[group]
        )

    small = [
        pltpu.make_async_copy(maps_hbm.at[0], maps_ref, sems.at[0]),
        pltpu.make_async_copy(part_hbm, part_ref, sems.at[1]),
        pltpu.make_async_copy(sampling_hbm, sampling_ref, sems.at[2]),
        pltpu.make_async_copy(tables_hbm, tables_ref, sems.at[3]),
    ]
    small[2].start()
    small[3].start()
    load(0).start()
    small[0].start()
    small[1].start()
    for group in range(1, groups):
        load(group).start()

    def part_maps():
        small[0].wait()
        small[1].wait()
        maps = maps_ref[...].reshape(rows, doubled)
        re = moved(maps[:, :half], part_ref[...])
        im = moved(maps[:, half:], part_ref[...])
        parted_ref[...] = cat(
            re[:, :quarter], im[:, :quarter], re[:, quarter:], im[:, quarter:]
        ).reshape(coils, readout, doubled)

    small[2].wait()
    small[3].wait()
    energy = jnp.zeros((readout, quarter), F32)
    for group in range(groups):
        load(group).wait()
        evens, odds = [], []
        count = GROUPS[group]
        for frame in range(ends[group], ends[group + 1]):
            data = data_ref[frame].reshape(rows, doubled)
            weight = sampling_ref[frame : frame + 1, :].astype(F32)
            low, high = weight[:, :quarter], weight[:, quarter:]
            re_low, re_high, im_low, im_high = quarters(data)
            re_low, re_high = re_low * low, re_high * high
            im_low, im_high = im_low * low, im_high * high
            evens.append(cat(re_low + re_high, im_low + im_high))
            odds.append(cat(re_low - re_high, im_low - im_high))
        evens = product(jnp.concatenate(evens, 0), tables_ref, 0)
        odds = product(jnp.concatenate(odds, 0), tables_ref, 2)
        evens = evens.reshape(count, coils, readout, half)
        odds = odds.reshape(count, coils, readout, half)
        if group == 0:
            part_maps()
        for index in range(count):
            image = cat(
                combine_coils(evens[index], parted_ref[:, :, :half]),
                combine_coils(odds[index], parted_ref[:, :, half:]),
            )
            image_ref[ends[group] + index] = image
            energy = energy + sum(piece * piece for piece in quarters(image))
    energy_ref[...] = jnp.broadcast_to(jnp.sum(energy), energy_ref.shape)
    send = pltpu.make_async_copy(energy_ref, energy_hbm, sems.at[4])
    send.start()
    image_x_ref[...] = jnp.swapaxes(image_ref[...], 0, 1)
    send.wait()


def normal_kernel(begin, image_ref, maps_ref, sampling_ref, tables_ref, *rest):
    out_ref = rest[-1]
    frames_here = out_ref.shape[0]
    coils, readout, doubled = maps_ref.shape
    half, quarter = doubled // 2, doubled // 4
    rows = coils * readout

    def lines(group, offset, table):
        pieces = []
        for index in range(NORMAL_STEP):
            frame = begin + group * NORMAL_STEP + index
            re = image_ref[frame, :, offset : offset + quarter][None]
            im = image_ref[frame, :, offset + quarter : offset + half][None]
            map_re = maps_ref[:, :, offset : offset + quarter]
            map_im = maps_ref[:, :, offset + quarter : offset + half]
            pieces.append(
                cat(map_re * re - map_im * im, map_re * im + map_im * re).reshape(rows, half)
            )
        return turned_product(jnp.concatenate(pieces, 0), tables_ref, table)

    def forth(group):
        from_even = lines(group, 0, 0)
        from_odd = lines(group, half, 2)
        low = from_even + from_odd
        high = from_even - from_odd
        evens, odds = [], []
        for index in range(NORMAL_STEP):
            frame = begin + group * NORMAL_STEP + index
            weight = sampling_ref[frame : frame + 1, :].astype(F32)
            weight_low = cat(weight[:, :quarter], weight[:, :quarter])
            weight_high = cat(weight[:, quarter:], weight[:, quarter:])
            kept_low = low[index * rows : (index + 1) * rows] * weight_low
            kept_high = high[index * rows : (index + 1) * rows] * weight_high
            evens.append(kept_low + kept_high)
            odds.append(kept_low - kept_high)
        return jnp.concatenate(evens, 0), jnp.concatenate(odds, 0)

    def back(group, evens, odds):
        evens = product(evens, tables_ref, 0).reshape(NORMAL_STEP, coils, readout, half)
        odds = product(odds, tables_ref, 2).reshape(NORMAL_STEP, coils, readout, half)
        for index in range(NORMAL_STEP):
            out_ref[group * NORMAL_STEP + index] = cat(
                combine_coils(evens[index], maps_ref[:, :, :half]),
                combine_coils(odds[index], maps_ref[:, :, half:]),
            )

    groups = frames_here // NORMAL_STEP
    held = forth(0)
    for group in range(groups):
        later = forth(group + 1) if group + 1 < groups else None
        back(group, *held)
        held = later


def lines_of(block):
    re_even, im_even, re_odd, im_odd = quarters(block)
    return cat(re_even, re_odd), cat(im_even, im_odd)


def frequencies(blocks, x, table):
    parts = [lines_of(block[x]) for block in blocks]
    return left_product(
        table, jnp.concatenate([part[0] for part in parts] + [part[1] for part in parts], 0)
    )


def level(energy_ref, cells):
    total = jnp.sum(energy_ref[...], axis=0, keepdims=True)
    return jnp.sqrt(total / cells + EPSILON)


def clip_time(dual, limit):
    size = dual.shape[0] // 2
    re, im = dual[:size], dual[size:]
    scale = jnp.minimum(1.0, limit * lax.rsqrt(re * re + im * im))
    return jnp.concatenate([re * scale, im * scale], 0)


def frames_of(dual, table):
    field = left_product(table, dual)
    size, half = field.shape[0] // 2, field.shape[1] // 2
    re, im = field[:size], field[size:]
    return cat(re[:, :half], im[:, :half], re[:, half:], im[:, half:])


def later_lines(field):
    re_even, im_even, re_odd, im_odd = quarters(field)
    size = re_even.shape[-1]
    last = lax.broadcasted_iota(jnp.int32, re_even.shape, 1) == size - 1

    def rolled(piece):
        return jnp.where(last, 0.0, pltpu.roll(piece, size - 1, 1))

    return cat(re_odd, im_odd, rolled(re_even), rolled(im_even))


def earlier_lines(field):
    re_even, im_even, re_odd, im_odd = quarters(field)
    first = lax.broadcasted_iota(jnp.int32, re_even.shape, 1) == 0

    def rolled(piece):
        return jnp.where(first, 0.0, pltpu.roll(piece, 1, 1))

    return cat(rolled(re_odd), rolled(im_odd), re_even, im_even)


def clip_space(components, limit):
    re_even, im_even, re_odd, im_odd = (
        sum(piece * piece for piece in pieces)
        for pieces in zip(*(quarters(component) for component in components))
    )
    even = jnp.minimum(1.0, limit * lax.rsqrt(re_even + im_even))
    odd = jnp.minimum(1.0, limit * lax.rsqrt(re_odd + im_odd))
    scale = cat(even, even, odd, odd)
    return [component * scale for component in components]


def space_step(field, above, x, old, limit):
    readout = field.shape[0]
    here = field[x]
    further = field[x + 1] if x + 1 < readout else jnp.zeros_like(here)
    increments = (above[x] - here, further - here, later_lines(here) - here)
    if old is None:
        duals = [SIGMA * increment for increment in increments]
    else:
        duals = [
            old[index, x] + SIGMA * increment for index, increment in enumerate(increments)
        ]
    return clip_space(duals, limit)


def around(near_ref, far_ref):
    even = lax.axis_index("cuts") % 2 == 0
    near, far = near_ref[...], far_ref[...]
    return jnp.where(even, near, far), jnp.where(even, far, near)


def space_part(own, above, below, x, rows_before, has_below, old, old_below, limit):
    duals = space_step(own, above, x, old, limit)
    duals_below = space_step(below, own, x, old_below, limit)
    total = has_below * duals_below[0] - duals[0]
    total = total + (rows_before - duals[1])
    total = total + (earlier_lines(duals[2]) - duals[2])
    return total, duals, duals_below


def in_turn(own_ref, one_ref, two_ref, three_ref):
    even = lax.axis_index("frame") % 2 == 0
    one, three = one_ref[...], three_ref[...]
    return own_ref, jnp.where(even, one, three), two_ref, jnp.where(even, three, one)


def time_duals(duals, level):
    limit = LAM_TIME * cat(level, level)
    return [clip_time(dual, limit) for dual in duals]


def summed_kernel(energy_ref, out_ref):
    out_ref[...] = jnp.broadcast_to(
        jnp.sum(energy_ref[...], axis=0, keepdims=True), out_ref.shape
    )


def frequency_kernel(own_ref, one_ref, two_ref, three_ref, fore_ref, out_ref):
    blocks = in_turn(own_ref, one_ref, two_ref, three_ref)
    for x in range(own_ref.shape[0]):
        out_ref[x] = SIGMA * frequencies(blocks, x, fore_ref[...])


def first_kernel(
    cells, energy_ref, own_ref, near_ref, far_ref, normal_ref, frequency_ref, back_ref,
    base_ref, bar_x_ref, bar_ref, dual_ref, level_ref, space_ref, space_below_ref,
):
    rms_level = level(energy_ref, cells)
    level_ref[...] = jnp.broadcast_to(rms_level, level_ref.shape)
    time = time_duals([frequency_ref[x] for x in range(frequency_ref.shape[0])], rms_level)
    for x, dual in enumerate(time):
        dual_ref[x] = dual
    fields = [frames_of(dual, back_ref[...]) for dual in time]
    limit_space = LAM_SPACE * rms_level
    has_below = (lax.axis_index("cuts") > 0).astype(F32)
    above, below = around(near_ref, far_ref)
    normal = jnp.swapaxes(normal_ref[...], 0, 1)
    rows_before = jnp.zeros(own_ref.shape[1:], F32)
    bars = []
    for x in range(own_ref.shape[0]):
        total, duals, duals_below = space_part(
            own_ref, above, below, x, rows_before, has_below, None, None, limit_space
        )
        rows_before = duals[1]
        for index in range(3):
            space_ref[index, x] = duals[index]
            space_below_ref[index, x] = duals_below[index]
        initial = own_ref[x]
        data_part = TAKE * (normal[x] - initial)
        updated = initial - TAU * (data_part + fields[x] + total)
        base_ref[x] = updated - TAU * (KEEP * data_part - TAKE * initial)
        bar = 2.0 * updated - initial
        bar_x_ref[x] = bar
        bars.append(bar)
    bar_ref[...] = jnp.swapaxes(jnp.stack(bars, 0), 0, 1)


def middle_kernel(
    level_ref, near_ref, far_ref, own_ref, two_ref, three_ref, normal_ref, base_ref, dual_ref,
    space_ref, space_below_ref, fore_ref,
    partial_ref, out_ref,
):
    absent = jnp.zeros(own_ref.shape, F32)
    blocks = in_turn(own_ref, absent, two_ref, three_ref)
    for x in range(own_ref.shape[0]):
        partial_ref[x] = dual_ref[x] + SIGMA * frequencies(blocks, x, fore_ref[...])
    limit_space = LAM_SPACE * level_ref[0:1, :]
    has_below = (lax.axis_index("cuts") > 0).astype(F32)
    above, below = around(near_ref, far_ref)
    normal = jnp.swapaxes(normal_ref[...], 0, 1)
    rows_before = jnp.zeros(own_ref.shape[1:], F32)
    for x in range(own_ref.shape[0]):
        total, duals, _ = space_part(
            own_ref, above, below, x, rows_before, has_below,
            space_ref, space_below_ref, limit_space,
        )
        rows_before = duals[1]
        out_ref[x] = base_ref[x] - TAU * (TAKE * normal[x] + total)


def last_kernel(
    level_ref, one_ref, partial_ref, base_ref, across_ref, back_ref, part_ref, out_ref
):
    places = range(one_ref.shape[0])
    across = across_ref[lax.axis_index("frame") % 2]
    duals = [
        partial_ref[x] + SIGMA * frequencies((one_ref,), x, across) for x in places
    ]
    duals = time_duals(duals, level_ref[0:1, :])
    images = [base_ref[x] - TAU * frames_of(duals[x], back_ref[...]) for x in places]
    image = jnp.concatenate(images, 0)
    re_even, im_even, re_odd, im_odd = quarters(image)
    image = cat(
        moved(cat(re_even, re_odd), part_ref[...]), moved(cat(im_even, im_odd), part_ref[...])
    )
    out_ref[:, 0] = jnp.swapaxes(image.reshape(one_ref.shape), 0, 1)


def stages(blocks, cuts):
    rows = 4 if cuts % 4 == 0 else 1
    index = np.arange(blocks * cuts).reshape(blocks * rows, cuts // rows)
    return index.T.tolist(), index.tolist()


def params():
    return pltpu.CompilerParams(vmem_limit_bytes=VMEM_BYTES)


def cost(flops, moved_bytes):
    return pl.CostEstimate(flops=flops, bytes_accessed=moved_bytes, transcendentals=0)


def struct(*shape):
    return jax.ShapeDtypeStruct(shape, F32)


def shards(measured, coil_maps, sampling):
    frames_here, slices_here, coils, readout, doubled = measured.shape
    positions = doubled // 2
    blocks = lax.axis_size("frame")
    slices_all = slices_here * lax.axis_size("cuts")
    frames_all = frames_here * blocks
    inner, outer = stages(blocks, lax.axis_size("cuts"))
    cells = float(frames_all * slices_all * readout * positions)
    tables = jnp.asarray(line_tables(positions))
    time_fore, time_back, time_across = (jnp.asarray(table) for table in time_tables(frames_all, frames_here))
    parting = parting_table(positions)
    part, unpart = jnp.asarray(parting, BF16), jnp.asarray(parting.T, BF16)
    plane = (readout, frames_here, doubled)
    turned = (frames_here, readout, doubled)
    rows = frames_here * coils * readout
    hbm = pl.BlockSpec(memory_space=pltpu.HBM)
    vmem = pl.BlockSpec(memory_space=pltpu.VMEM)

    initial, initial_x, energy, maps, tables, sampling = pl.pallas_call(
        initial_kernel,
        in_specs=[hbm] * 5,
        out_specs=[vmem] * 2 + [pl.BlockSpec(memory_space=pl.ANY)] + [vmem] * 3,
        out_shape=[
            struct(*turned), struct(*plane), struct(len(inner[0]), 128),
            pltpu.VMEM((coils, readout, doubled), F32),
            pltpu.VMEM(tables.shape, BF16),
            pltpu.VMEM(sampling.shape, jnp.int32),
        ],
        scratch_shapes=[
            pltpu.VMEM((frames_here, coils, readout, doubled), F32),
            pltpu.VMEM((coils, readout, doubled), F32),
            pltpu.VMEM(part.shape, BF16),
            pltpu.VMEM((len(inner[0]), 128), F32),
            pltpu.SemaphoreType.DMA((len(GROUPS),)),
            pltpu.SemaphoreType.DMA((5,)),
        ],
        compiler_params=params(),
        cost_estimate=cost(6 * rows * doubled * positions, measured.size * 4),
    )(*(
        pltpu.with_memory_space_constraint(array, pltpu.HBM)
        for array in (measured, coil_maps, sampling, tables, part)
    ))

    def normal(image, begin=0, count=frames_here, after=()):
        def kernel(*refs):
            normal_kernel(begin, *refs)

        return pl.pallas_call(
            kernel,
            in_specs=[vmem] * (4 + len(after)),
            out_specs=vmem,
            out_shape=struct(count, readout, doubled),
            compiler_params=params(),
            cost_estimate=cost(12 * rows * doubled * positions * count // frames_here, 1000000),
        )(image, *(
            pltpu.with_memory_space_constraint(array, pltpu.VMEM)
            for array in (maps, sampling, tables)
        ), *after)

    def swapped(image, by):
        return lax.ppermute(image, "frame", [(index, index ^ by) for index in range(blocks)])

    def gathered(image):
        return [image] + [swapped(image, by) for by in range(1, blocks)]

    def neighbours(image):
        count = lax.axis_size("cuts")
        pairs = [[(i, i ^ 1) for i in range(count)], [(i, ((i + 1) ^ 1) - 1) for i in range(1, count - 1)]]
        return [lax.ppermute(image, "cuts", pair) for pair in pairs]


    def call(kernel, args, out_shape, flops):
        return pl.pallas_call(
            kernel,
            in_specs=[vmem] * len(args),
            out_specs=jax.tree.map(lambda _: vmem, out_shape),
            out_shape=out_shape,
            compiler_params=params(),
            cost_estimate=cost(flops, sum(arg.size * 4 for arg in args)),
        )(*args)

    energies = lax.all_to_all(energy, AXES, 0, 0, tiled=True, axis_index_groups=inner)
    energies = call(summed_kernel, [energies], pltpu.VMEM((len(outer[0]), 128), F32), 1000)
    energies = lax.all_to_all(energies, AXES, 0, 0, tiled=True, axis_index_groups=outer)

    time_flops = 7 * (2 * frames_all) ** 2 * readout * positions
    dual_shape = struct(readout, 2 * frames_all, positions)
    duals_shape = struct(3, *plane)

    def first(*refs):
        first_kernel(cells, *refs)

    all_blocks = gathered(initial_x)
    pair_near, pair_far = neighbours(initial_x)
    normal_initial = normal(initial)
    frequency = call(frequency_kernel, all_blocks + [time_fore], dual_shape, time_flops // 2)
    base, bar_x, bar, time_dual, rms_level, space_dual, space_below = call(
        first,
        [energies, initial_x, pair_near, pair_far, normal_initial, frequency, time_back],
        [
            struct(*plane), struct(*plane), struct(*turned), dual_shape, struct(8, 128),
            duals_shape, duals_shape,
        ],
        time_flops // 2,
    )
    one, two, three = gathered(bar_x)[1:]
    pair_near, pair_far = neighbours(bar_x)
    normal_bar = normal(bar)
    partial, base = call(
        middle_kernel,
        [
            rms_level, pair_near, pair_far, bar_x, two, three, normal_bar, base, time_dual,
            space_dual, space_below, time_fore,
        ],
        [dual_shape, struct(*plane)],
        time_flops // 2,
    )
    return call(
        last_kernel,
        [rms_level, one, partial, base, time_across, time_back, unpart],
        struct(frames_here, slices_here, readout, doubled),
        time_flops // 2,
    )


def solution(mesh):
    placed = (P("frame", "cuts", None, None, None), P("cuts", None, None, None), P("frame", None))
    return jax.shard_map(
        shards,
        mesh=mesh,
        in_specs=placed,
        out_specs=P("frame", "cuts", None, None),
        check_vma=False,
    )
```

```python
import math

import jax
import jax.numpy as jnp
import numpy as np
from jax import lax
from jax.experimental import pallas as pl
from jax.experimental.pallas import tpu as pltpu
from jax.sharding import PartitionSpec as P

ITERS = 2


TAU = 0.25
SIGMA = 0.25
LAM_TIME = 0.2
LAM_SPACE = 0.1
EPSILON = 1e-06
KEEP = 1.0 / (1.0 + SIGMA)
TAKE = SIGMA / (1.0 + SIGMA)
AXES = ("frame", "cuts")
GROUPS = (4, 6, 6)
NORMAL_STEP = 4
VMEM_BYTES = 24 * 1024 * 1024
BF16 = jnp.bfloat16
F32 = jnp.float32


def split_table(table):
    high = table.astype(np.float32).astype(BF16)
    low = (table - high.astype(np.float64)).astype(np.float32).astype(BF16)
    return high, low


def block_table(cosine, sine):
    return np.concatenate(
        [np.concatenate([cosine, sine], 1), np.concatenate([-sine, cosine], 1)], 0
    )


def line_tables(positions):
    half = positions // 2
    lines = np.arange(half)[:, None]
    backs = []
    for places in (2 * np.arange(half), 2 * np.arange(half) + 1):
        angles = 2.0 * math.pi / positions * (lines * places[None, :] % positions)
        back = block_table(np.cos(angles), np.sin(angles)) / math.sqrt(positions)
        backs.extend(split_table(back))
    return np.stack(backs, 0)


def time_tables(frames_all, frames_here):
    index = np.arange(frames_all)
    angles = 2.0 * math.pi / frames_all * (index[:, None] * index[None, :] % frames_all)
    fore = block_table(np.cos(angles), np.sin(angles)) / math.sqrt(frames_all)
    rows = np.concatenate([np.arange(frames_here), frames_all + np.arange(frames_here)])
    out = []
    last = frames_all // frames_here - 1
    for table in (fore, fore.T[rows], fore[:, rows + frames_here], fore[:, rows + last * frames_here]):
        high, low = split_table(table)
        out.append(np.concatenate([high, high, low], 1))
    return out[0], out[1], np.stack(out[2:], 0)


def parting_table(positions):
    table = np.zeros((positions, positions), np.float32)
    half = positions // 2
    table[2 * np.arange(half), np.arange(half)] = 1.0
    table[2 * np.arange(half) + 1, half + np.arange(half)] = 1.0
    return table


def parted(value):
    high = value.astype(BF16)
    return high, (value - high.astype(F32)).astype(BF16)


def product(value, tables_ref, index):
    high, low = parted(value)
    table_high, table_low = tables_ref[index], tables_ref[index + 1]
    return jnp.dot(
        jnp.concatenate([high, low, high], -1),
        jnp.concatenate([table_high, table_high, table_low], 0),
        preferred_element_type=F32,
    )


def turned_product(value, tables_ref, index):
    high, low = parted(value)
    table_high, table_low = tables_ref[index], tables_ref[index + 1]
    return lax.dot_general(
        jnp.concatenate([high, low, high], -1),
        jnp.concatenate([table_high, table_high, table_low], -1),
        (((1,), (1,)), ((), ())),
        preferred_element_type=F32,
    )


def left_product(table, value):
    high, low = parted(value)
    return jnp.dot(
        table, jnp.concatenate([high, low, high], 0), preferred_element_type=F32
    )


def moved(value, table):
    first = value.astype(BF16)
    rest = value - first.astype(F32)
    second = rest.astype(BF16)
    third = (rest - second.astype(F32)).astype(BF16)
    return sum(
        jnp.dot(piece, table, preferred_element_type=F32) for piece in (first, second, third)
    )


def quarters(value):
    size = value.shape[-1] // 4
    return [value[..., index * size : (index + 1) * size] for index in range(4)]


def cat(*pieces):
    return jnp.concatenate(pieces, -1)


def combine_coils(coil_fields, maps):
    re, im = coil_fields[..., :128], coil_fields[..., 128:]
    map_re, map_im = maps[..., :128], maps[..., 128:]
    return cat(
        jnp.sum(map_re * re + map_im * im, axis=0), jnp.sum(map_re * im - map_im * re, axis=0)
    )


def initial_kernel(
    measured_hbm, maps_hbm, sampling_hbm, tables_hbm, part_hbm,
    image_ref, image_x_ref, energy_hbm, parted_ref, tables_ref, sampling_ref,
    data_ref, maps_ref, part_ref, energy_ref, data_sem, sems,
):
    frames_here, coils, readout, doubled = data_ref.shape
    half, quarter = doubled // 2, doubled // 4
    rows = coils * readout
    ends = [sum(GROUPS[:i]) for i in range(len(GROUPS) + 1)]
    groups = len(GROUPS)

    def load(group):
        frames = pl.ds(ends[group], GROUPS[group])
        return pltpu.make_async_copy(
            measured_hbm.at[frames, 0], data_ref.at[frames], data_sem.at[group]
        )

    small = [
        pltpu.make_async_copy(maps_hbm.at[0], maps_ref, sems.at[0]),
        pltpu.make_async_copy(part_hbm, part_ref, sems.at[1]),
        pltpu.make_async_copy(sampling_hbm, sampling_ref, sems.at[2]),
        pltpu.make_async_copy(tables_hbm, tables_ref, sems.at[3]),
    ]
    small[2].start()
    small[3].start()
    load(0).start()
    small[0].start()
    small[1].start()
    for group in range(1, groups):
        load(group).start()

    def part_maps():
        small[0].wait()
        small[1].wait()
        maps = maps_ref[...].reshape(rows, doubled)
        re = moved(maps[:, :half], part_ref[...])
        im = moved(maps[:, half:], part_ref[...])
        parted_ref[...] = cat(
            re[:, :quarter], im[:, :quarter], re[:, quarter:], im[:, quarter:]
        ).reshape(coils, readout, doubled)

    small[2].wait()
    small[3].wait()
    energy = jnp.zeros((readout, quarter), F32)
    for group in range(groups):
        load(group).wait()
        evens, odds = [], []
        count = GROUPS[group]
        for frame in range(ends[group], ends[group + 1]):
            data = data_ref[frame].reshape(rows, doubled)
            weight = sampling_ref[frame : frame + 1, :].astype(F32)
            low, high = weight[:, :quarter], weight[:, quarter:]
            re_low, re_high, im_low, im_high = quarters(data)
            re_low, re_high = re_low * low, re_high * high
            im_low, im_high = im_low * low, im_high * high
            evens.append(cat(re_low + re_high, im_low + im_high))
            odds.append(cat(re_low - re_high, im_low - im_high))
        evens = product(jnp.concatenate(evens, 0), tables_ref, 0)
        odds = product(jnp.concatenate(odds, 0), tables_ref, 2)
        evens = evens.reshape(count, coils, readout, half)
        odds = odds.reshape(count, coils, readout, half)
        if group == 0:
            part_maps()
        for index in range(count):
            image = cat(
                combine_coils(evens[index], parted_ref[:, :, :half]),
                combine_coils(odds[index], parted_ref[:, :, half:]),
            )
            image_ref[ends[group] + index] = image
            energy = energy + sum(piece * piece for piece in quarters(image))
    energy_ref[...] = jnp.broadcast_to(jnp.sum(energy), energy_ref.shape)
    send = pltpu.make_async_copy(energy_ref, energy_hbm, sems.at[4])
    send.start()
    image_x_ref[...] = jnp.swapaxes(image_ref[...], 0, 1)
    send.wait()


def normal_kernel(begin, image_ref, maps_ref, sampling_ref, tables_ref, *rest):
    out_ref = rest[-1]
    frames_here = out_ref.shape[0]
    coils, readout, doubled = maps_ref.shape
    half, quarter = doubled // 2, doubled // 4
    rows = coils * readout

    def lines(group, offset, table):
        pieces = []
        for index in range(NORMAL_STEP):
            frame = begin + group * NORMAL_STEP + index
            re = image_ref[frame, :, offset : offset + quarter][None]
            im = image_ref[frame, :, offset + quarter : offset + half][None]
            map_re = maps_ref[:, :, offset : offset + quarter]
            map_im = maps_ref[:, :, offset + quarter : offset + half]
            pieces.append(
                cat(map_re * re - map_im * im, map_re * im + map_im * re).reshape(rows, half)
            )
        return turned_product(jnp.concatenate(pieces, 0), tables_ref, table)

    def forth(group):
        from_even = lines(group, 0, 0)
        from_odd = lines(group, half, 2)
        low = from_even + from_odd
        high = from_even - from_odd
        evens, odds = [], []
        for index in range(NORMAL_STEP):
            frame = begin + group * NORMAL_STEP + index
            weight = sampling_ref[frame : frame + 1, :].astype(F32)
            weight_low = cat(weight[:, :quarter], weight[:, :quarter])
            weight_high = cat(weight[:, quarter:], weight[:, quarter:])
            kept_low = low[index * rows : (index + 1) * rows] * weight_low
            kept_high = high[index * rows : (index + 1) * rows] * weight_high
            evens.append(kept_low + kept_high)
            odds.append(kept_low - kept_high)
        return jnp.concatenate(evens, 0), jnp.concatenate(odds, 0)

    def back(group, evens, odds):
        evens = product(evens, tables_ref, 0).reshape(NORMAL_STEP, coils, readout, half)
        odds = product(odds, tables_ref, 2).reshape(NORMAL_STEP, coils, readout, half)
        for index in range(NORMAL_STEP):
            out_ref[group * NORMAL_STEP + index] = cat(
                combine_coils(evens[index], maps_ref[:, :, :half]),
                combine_coils(odds[index], maps_ref[:, :, half:]),
            )

    groups = frames_here // NORMAL_STEP
    held = forth(0)
    for group in range(groups):
        later = forth(group + 1) if group + 1 < groups else None
        back(group, *held)
        held = later


def lines_of(block):
    re_even, im_even, re_odd, im_odd = quarters(block)
    return cat(re_even, re_odd), cat(im_even, im_odd)


def frequencies(blocks, x, table):
    parts = [lines_of(block[x]) for block in blocks]
    return left_product(
        table, jnp.concatenate([part[0] for part in parts] + [part[1] for part in parts], 0)
    )


def level(energy_ref, cells):
    total = jnp.sum(energy_ref[...], axis=0, keepdims=True)
    return jnp.sqrt(total / cells + EPSILON)


def clip_time(dual, limit):
    size = dual.shape[0] // 2
    re, im = dual[:size], dual[size:]
    scale = jnp.minimum(1.0, limit * lax.rsqrt(re * re + im * im))
    return jnp.concatenate([re * scale, im * scale], 0)


def frames_of(dual, table):
    field = left_product(table, dual)
    size, half = field.shape[0] // 2, field.shape[1] // 2
    re, im = field[:size], field[size:]
    return cat(re[:, :half], im[:, :half], re[:, half:], im[:, half:])


def later_lines(field):
    re_even, im_even, re_odd, im_odd = quarters(field)
    size = re_even.shape[-1]
    last = lax.broadcasted_iota(jnp.int32, re_even.shape, 1) == size - 1

    def rolled(piece):
        return jnp.where(last, 0.0, pltpu.roll(piece, size - 1, 1))

    return cat(re_odd, im_odd, rolled(re_even), rolled(im_even))


def earlier_lines(field):
    re_even, im_even, re_odd, im_odd = quarters(field)
    first = lax.broadcasted_iota(jnp.int32, re_even.shape, 1) == 0

    def rolled(piece):
        return jnp.where(first, 0.0, pltpu.roll(piece, 1, 1))

    return cat(rolled(re_odd), rolled(im_odd), re_even, im_even)


def clip_space(components, limit):
    re_even, im_even, re_odd, im_odd = (
        sum(piece * piece for piece in pieces)
        for pieces in zip(*(quarters(component) for component in components))
    )
    even = jnp.minimum(1.0, limit * lax.rsqrt(re_even + im_even))
    odd = jnp.minimum(1.0, limit * lax.rsqrt(re_odd + im_odd))
    scale = cat(even, even, odd, odd)
    return [component * scale for component in components]


def space_step(field, above, x, old, limit):
    readout = field.shape[0]
    here = field[x]
    further = field[x + 1] if x + 1 < readout else jnp.zeros_like(here)
    increments = (above[x] - here, further - here, later_lines(here) - here)
    if old is None:
        duals = [SIGMA * increment for increment in increments]
    else:
        duals = [
            old[index, x] + SIGMA * increment for index, increment in enumerate(increments)
        ]
    return clip_space(duals, limit)


def around(near_ref, far_ref):
    even = lax.axis_index("cuts") % 2 == 0
    near, far = near_ref[...], far_ref[...]
    return jnp.where(even, near, far), jnp.where(even, far, near)


def space_part(own, above, below, x, rows_before, has_below, old, old_below, limit):
    duals = space_step(own, above, x, old, limit)
    duals_below = space_step(below, own, x, old_below, limit)
    total = has_below * duals_below[0] - duals[0]
    total = total + (rows_before - duals[1])
    total = total + (earlier_lines(duals[2]) - duals[2])
    return total, duals, duals_below


def in_turn(own_ref, one_ref, two_ref, three_ref):
    even = lax.axis_index("frame") % 2 == 0
    one, three = one_ref[...], three_ref[...]
    return own_ref, jnp.where(even, one, three), two_ref, jnp.where(even, three, one)


def time_duals(duals, level):
    limit = LAM_TIME * cat(level, level)
    return [clip_time(dual, limit) for dual in duals]


def summed_kernel(energy_ref, out_ref):
    out_ref[...] = jnp.broadcast_to(
        jnp.sum(energy_ref[...], axis=0, keepdims=True), out_ref.shape
    )


def frequency_kernel(own_ref, one_ref, two_ref, three_ref, fore_ref, out_ref):
    blocks = in_turn(own_ref, one_ref, two_ref, three_ref)
    for x in range(own_ref.shape[0]):
        out_ref[x] = SIGMA * frequencies(blocks, x, fore_ref[...])


def first_kernel(
    cells, energy_ref, own_ref, near_ref, far_ref, normal_ref, frequency_ref, back_ref,
    base_ref, bar_x_ref, bar_ref, dual_ref, level_ref, space_ref, space_below_ref,
):
    rms_level = level(energy_ref, cells)
    level_ref[...] = jnp.broadcast_to(rms_level, level_ref.shape)
    time = time_duals([frequency_ref[x] for x in range(frequency_ref.shape[0])], rms_level)
    for x, dual in enumerate(time):
        dual_ref[x] = dual
    fields = [frames_of(dual, back_ref[...]) for dual in time]
    limit_space = LAM_SPACE * rms_level
    has_below = (lax.axis_index("cuts") > 0).astype(F32)
    above, below = around(near_ref, far_ref)
    normal = jnp.swapaxes(normal_ref[...], 0, 1)
    rows_before = jnp.zeros(own_ref.shape[1:], F32)
    bars = []
    for x in range(own_ref.shape[0]):
        total, duals, duals_below = space_part(
            own_ref, above, below, x, rows_before, has_below, None, None, limit_space
        )
        rows_before = duals[1]
        for index in range(3):
            space_ref[index, x] = duals[index]
            space_below_ref[index, x] = duals_below[index]
        initial = own_ref[x]
        data_part = TAKE * (normal[x] - initial)
        updated = initial - TAU * (data_part + fields[x] + total)
        base_ref[x] = updated - TAU * (KEEP * data_part - TAKE * initial)
        bar = 2.0 * updated - initial
        bar_x_ref[x] = bar
        bars.append(bar)
    bar_ref[...] = jnp.swapaxes(jnp.stack(bars, 0), 0, 1)


def middle_kernel(
    level_ref, near_ref, far_ref, own_ref, three_ref, two_ref, normal_ref, base_ref, dual_ref,
    space_ref, space_below_ref, fore_ref,
    partial_ref, out_ref,
):
    absent = jnp.zeros(own_ref.shape, F32)
    blocks = in_turn(own_ref, absent, two_ref, three_ref)
    for x in range(own_ref.shape[0]):
        partial_ref[x] = dual_ref[x] + SIGMA * frequencies(blocks, x, fore_ref[...])
    limit_space = LAM_SPACE * level_ref[0:1, :]
    has_below = (lax.axis_index("cuts") > 0).astype(F32)
    above, below = around(near_ref, far_ref)
    normal = jnp.swapaxes(normal_ref[...], 0, 1)
    rows_before = jnp.zeros(own_ref.shape[1:], F32)
    for x in range(own_ref.shape[0]):
        total, duals, _ = space_part(
            own_ref, above, below, x, rows_before, has_below,
            space_ref, space_below_ref, limit_space,
        )
        rows_before = duals[1]
        out_ref[x] = base_ref[x] - TAU * (TAKE * normal[x] + total)


def last_kernel(
    level_ref, one_ref, partial_ref, base_ref, across_ref, back_ref, part_ref, out_ref
):
    places = range(one_ref.shape[0])
    across = across_ref[lax.axis_index("frame") % 2]
    duals = [
        partial_ref[x] + SIGMA * frequencies((one_ref,), x, across) for x in places
    ]
    duals = time_duals(duals, level_ref[0:1, :])
    images = [base_ref[x] - TAU * frames_of(duals[x], back_ref[...]) for x in places]
    image = jnp.concatenate(images, 0)
    re_even, im_even, re_odd, im_odd = quarters(image)
    image = cat(
        moved(cat(re_even, re_odd), part_ref[...]), moved(cat(im_even, im_odd), part_ref[...])
    )
    out_ref[:, 0] = jnp.swapaxes(image.reshape(one_ref.shape), 0, 1)


def stages(blocks, cuts):
    rows = 4 if cuts % 4 == 0 else 1
    index = np.arange(blocks * cuts).reshape(blocks * rows, cuts // rows)
    return index.T.tolist(), index.tolist()


def params():
    return pltpu.CompilerParams(vmem_limit_bytes=VMEM_BYTES)


def cost(flops, moved_bytes):
    return pl.CostEstimate(flops=flops, bytes_accessed=moved_bytes, transcendentals=0)


def struct(*shape):
    return jax.ShapeDtypeStruct(shape, F32)


def shards(measured, coil_maps, sampling):
    frames_here, slices_here, coils, readout, doubled = measured.shape
    positions = doubled // 2
    blocks = lax.axis_size("frame")
    slices_all = slices_here * lax.axis_size("cuts")
    frames_all = frames_here * blocks
    inner, outer = stages(blocks, lax.axis_size("cuts"))
    cells = float(frames_all * slices_all * readout * positions)
    tables = jnp.asarray(line_tables(positions))
    time_fore, time_back, time_across = (jnp.asarray(table) for table in time_tables(frames_all, frames_here))
    parting = parting_table(positions)
    part, unpart = jnp.asarray(parting, BF16), jnp.asarray(parting.T, BF16)
    plane = (readout, frames_here, doubled)
    turned = (frames_here, readout, doubled)
    rows = frames_here * coils * readout
    hbm = pl.BlockSpec(memory_space=pltpu.HBM)
    vmem = pl.BlockSpec(memory_space=pltpu.VMEM)

    initial, initial_x, energy, maps, tables, sampling = pl.pallas_call(
        initial_kernel,
        in_specs=[hbm] * 5,
        out_specs=[vmem] * 2 + [pl.BlockSpec(memory_space=pl.ANY)] + [vmem] * 3,
        out_shape=[
            struct(*turned), struct(*plane), struct(len(inner[0]), 128),
            pltpu.VMEM((coils, readout, doubled), F32),
            pltpu.VMEM(tables.shape, BF16),
            pltpu.VMEM(sampling.shape, jnp.int32),
        ],
        scratch_shapes=[
            pltpu.VMEM((frames_here, coils, readout, doubled), F32),
            pltpu.VMEM((coils, readout, doubled), F32),
            pltpu.VMEM(part.shape, BF16),
            pltpu.VMEM((len(inner[0]), 128), F32),
            pltpu.SemaphoreType.DMA((len(GROUPS),)),
            pltpu.SemaphoreType.DMA((5,)),
        ],
        compiler_params=params(),
        cost_estimate=cost(6 * rows * doubled * positions, measured.size * 4),
    )(*(
        pltpu.with_memory_space_constraint(array, pltpu.HBM)
        for array in (measured, coil_maps, sampling, tables, part)
    ))

    def normal(image, begin=0, count=frames_here, after=()):
        def kernel(*refs):
            normal_kernel(begin, *refs)

        return pl.pallas_call(
            kernel,
            in_specs=[vmem] * (4 + len(after)),
            out_specs=vmem,
            out_shape=struct(count, readout, doubled),
            compiler_params=params(),
            cost_estimate=cost(12 * rows * doubled * positions * count // frames_here, 1000000),
        )(image, *(
            pltpu.with_memory_space_constraint(array, pltpu.VMEM)
            for array in (maps, sampling, tables)
        ), *after)

    def swapped(image, by):
        return lax.ppermute(image, "frame", [(index, index ^ by) for index in range(blocks)])

    def gathered(image):
        return [image] + [swapped(image, by) for by in range(1, blocks)]

    def neighbours(image):
        count = lax.axis_size("cuts")
        pairs = [[(i, i ^ 1) for i in range(count)], [(i, ((i + 1) ^ 1) - 1) for i in range(1, count - 1)]]
        return [lax.ppermute(image, "cuts", pair) for pair in pairs]


    def call(kernel, args, out_shape, flops):
        return pl.pallas_call(
            kernel,
            in_specs=[vmem] * len(args),
            out_specs=jax.tree.map(lambda _: vmem, out_shape),
            out_shape=out_shape,
            compiler_params=params(),
            cost_estimate=cost(flops, sum(arg.size * 4 for arg in args)),
        )(*args)

    energies = lax.all_to_all(energy, AXES, 0, 0, tiled=True, axis_index_groups=inner)
    energies = call(summed_kernel, [energies], pltpu.VMEM((len(outer[0]), 128), F32), 1000)
    energies = lax.all_to_all(energies, AXES, 0, 0, tiled=True, axis_index_groups=outer)

    time_flops = 7 * (2 * frames_all) ** 2 * readout * positions
    dual_shape = struct(readout, 2 * frames_all, positions)
    duals_shape = struct(3, *plane)

    def first(*refs):
        first_kernel(cells, *refs)

    all_blocks = gathered(initial_x)
    pair_near, pair_far = neighbours(initial_x)
    normal_initial = normal(initial)
    frequency = call(frequency_kernel, all_blocks + [time_fore], dual_shape, time_flops // 2)
    base, bar_x, bar, time_dual, rms_level, space_dual, space_below = call(
        first,
        [energies, initial_x, pair_near, pair_far, normal_initial, frequency, time_back],
        [
            struct(*plane), struct(*plane), struct(*turned), dual_shape, struct(8, 128),
            duals_shape, duals_shape,
        ],
        time_flops // 2,
    )
    one, two, three = gathered(bar_x)[1:]
    pair_near, pair_far = neighbours(bar_x)
    normal_bar = normal(bar)
    partial, base = call(
        middle_kernel,
        [
            rms_level, pair_near, pair_far, bar_x, three, two, normal_bar, base, time_dual,
            space_dual, space_below, time_fore,
        ],
        [dual_shape, struct(*plane)],
        time_flops // 2,
    )
    return call(
        last_kernel,
        [rms_level, one, partial, base, time_across, time_back, unpart],
        struct(frames_here, slices_here, readout, doubled),
        time_flops // 2,
    )


def solution(mesh):
    placed = (P("frame", "cuts", None, None, None), P("cuts", None, None, None), P("frame", None))
    return jax.shard_map(
        shards,
        mesh=mesh,
        in_specs=placed,
        out_specs=P("frame", "cuts", None, None),
        check_vma=False,
    )
```
